512 devices in a mesh: pts: 256 (over x, y, z), rep: 2 (over core).
Axes of the slice: x: 4, y: 4, z: 16, core: 2. Of those that a mesh axis runs over, the one named last changes fastest.
Arguments:
- points: bfloat16 [262144, 256], P(('pts', 'rep')), may hold values from -6 to 6
- out_grad: bfloat16 [262144, 256], P(('pts', 'rep')), may hold values from -8 to 8
- ln_gain: float32 [256], replicated, may hold values from 0.5 to 1.5
- ln_bias: float32 [256], replicated, may hold values from -3 to 3
- w_mid: bfloat16 [256, 256], replicated, may hold values from -0.375 to 0.375
- w_feat: bfloat16 [256, 256], replicated, may hold values from -0.375 to 0.375
- w_slice: bfloat16 [32, 64], replicated, may hold values from -1 to 1
- temper: float32 [8], replicated, may hold values from 0.3 to 1.5
- query_weight: float32 [32, 32], replicated, may hold values from -1 to 1
- key_weight: float32 [32, 32], replicated, may hold values from -1 to 1
- value_weight: float32 [32, 32], replicated, may hold values from -1 to 1
- w_out: bfloat16 [256, 256], replicated, may hold values from -0.375 to 0.375
Outputs:
- grad_points: bfloat16 [262144, 256], P(('pts', 'rep'))
- grad_gain: float32 [256], replicated
- grad_bias: float32 [256], replicated
- grad_mid: float32 [256, 256], P('rep')
- grad_feat: float32 [256, 256], P('rep')
- grad_slice: float32 [32, 64], replicated
- grad_temper: float32 [8], replicated
- grad_query: float32 [32, 32], replicated
- grad_key: float32 [32, 32], replicated
- grad_value: float32 [32, 32], replicated
- output_weight_gradient: float32 [256, 256], P('rep')
The draws below stay inside these ranges and needn't reach their ends.
All inputs are finite; a program needn't handle non-finite values.
Results may differ from the reference program's by a relative error of at most 0.013.
The reference program's roundings to bfloat16 on the way count: a program that leaves them out, or rounds other values in their place, can miss the bound.
Values sent between devices are 32-bit elements; how exact they have to be, the bound alone decides.
A program may use at most 64 MiB of HBM per device.

```python
import math
import jax
import jax.numpy as jnp
from jax import lax

MODEL_WIDTH = 256
HEADS = 8
SLICES = 64
HEAD_DIM = 32
DEVICE_POINTS = 512
TOTAL_POINTS = 262144


def draw_points(key, part):
    key = jax.random.fold_in(key, 11)
    block_key, noise_key = jax.random.split(key, 2)
    block_count = TOTAL_POINTS // DEVICE_POINTS
    block_dirs = jnp.clip(jax.random.normal(block_key, (block_count, MODEL_WIDTH), jnp.float32), -2.5, 2.5)
    shared = jnp.repeat(block_dirs, DEVICE_POINTS, axis=0)
    noise = jnp.clip(jax.random.normal(noise_key, (TOTAL_POINTS, MODEL_WIDTH), jnp.float32), -4.0, 4.0)
    values = 2.5 * shared + noise
    return jnp.clip(values, -6.0, 6.0).astype(jnp.bfloat16)


def draw_out_grad(key, part):
    key = jax.random.fold_in(key, 7)
    block_key, noise_key = jax.random.split(key, 2)
    block_count = TOTAL_POINTS // DEVICE_POINTS
    row_index = jnp.arange(TOTAL_POINTS, dtype=jnp.float32)
    rising = 1.0 + 2.0 * row_index / max(TOTAL_POINTS - 1, 1)
    block_dirs = jnp.clip(jax.random.normal(block_key, (block_count, MODEL_WIDTH), jnp.float32), -2.5, 2.5)
    shared = jnp.repeat(block_dirs, DEVICE_POINTS, axis=0)
    noise = jnp.clip(jax.random.normal(noise_key, (TOTAL_POINTS, MODEL_WIDTH), jnp.float32), -4.0, 4.0)
    gradient = 0.7 * rising[:, None] * shared + 0.6 * noise
    return gradient.astype(jnp.bfloat16)


def normal_values(own_key, shape, deviation, most, held_as=jnp.bfloat16):
    entries = jax.random.normal(own_key, shape, jnp.float32) * deviation
    return jnp.minimum(jnp.maximum(entries, -most), most).astype(held_as)


def setup_inputs(seed: int = 0) -> dict:
    keys = jax.random.split(jax.random.key(seed), 13)
    points = draw_points(jax.random.fold_in(keys[12], 71), 0)
    out_grad = draw_out_grad(jax.random.fold_in(keys[12], 71), 0)
    ln_gain = jnp.clip(1.0 + 0.1 * jax.random.normal(keys[2], (MODEL_WIDTH,), jnp.float32), 0.5, 1.5)
    ln_bias = normal_values(keys[3], (MODEL_WIDTH,), 0.5, 3.0, jnp.float32)
    w_mid = normal_values(keys[4], (MODEL_WIDTH, MODEL_WIDTH), MODEL_WIDTH ** -0.5, 0.375)
    w_feat = normal_values(keys[5], (MODEL_WIDTH, MODEL_WIDTH), MODEL_WIDTH ** -0.5, 0.375)
    w_slice = normal_values(keys[6], (HEAD_DIM, SLICES), HEAD_DIM ** -0.5, 1.0)
    temper = jnp.clip(jnp.exp(jax.random.uniform(keys[7], (HEADS,), jnp.float32, math.log(0.3), math.log(1.5))), 0.3, 1.5)
    query_weight = normal_values(keys[8], (HEAD_DIM, HEAD_DIM), HEAD_DIM ** -0.5, 1.0, jnp.float32)
    key_weight = normal_values(keys[9], (HEAD_DIM, HEAD_DIM), HEAD_DIM ** -0.5, 1.0, jnp.float32)
    value_weight = normal_values(keys[10], (HEAD_DIM, HEAD_DIM), HEAD_DIM ** -0.5, 1.0, jnp.float32)
    w_out = normal_values(keys[11], (MODEL_WIDTH, MODEL_WIDTH), MODEL_WIDTH ** -0.5, 0.375)
    return {"points": points, "out_grad": out_grad, "ln_gain": ln_gain, "ln_bias": ln_bias, "w_mid": w_mid, "w_feat": w_feat, "w_slice": w_slice, "temper": temper, "query_weight": query_weight, "key_weight": key_weight, "value_weight": value_weight, "w_out": w_out}


def layer_norm(values, ln_gain, ln_bias):
    center = values - lax.optimization_barrier(jnp.mean(values, axis=-1, keepdims=True))
    spread = lax.optimization_barrier(jnp.mean(center * center, axis=-1, keepdims=True))
    return center * lax.rsqrt(spread + 1e-05) * ln_gain + ln_bias

def token_mix(slice_tokens, query_weight, key_weight, value_weight):
    highest_precision = lax.Precision.HIGHEST
    query_rows = jnp.einsum('ytj,jv->ytv', slice_tokens, query_weight, precision=highest_precision)
    slice_key_rows = jnp.einsum('ytj,jv->ytv', slice_tokens, key_weight, precision=highest_precision)
    slice_value_rows = jnp.einsum('ytj,jv->ytv', slice_tokens, value_weight, precision=highest_precision)
    scores = jnp.einsum('hme,hne->hmn', query_rows, slice_key_rows, precision=highest_precision) * slice_tokens.shape[-1] ** (-0.5)
    powers = jnp.exp(scores)
    attention = powers / lax.optimization_barrier(jnp.sum(powers, axis=-1, keepdims=True))
    return jnp.einsum('hmn,hne->hme', attention, slice_value_rows, precision=highest_precision)

def reference(points, out_grad, ln_gain, ln_bias, w_mid, w_feat, w_slice, temper, query_weight, key_weight, value_weight, w_out):
    highest_precision = lax.Precision.HIGHEST
    blocks = TOTAL_POINTS // DEVICE_POINTS
    point_blocks = points.reshape(blocks, DEVICE_POINTS, MODEL_WIDTH)
    grad_blocks = out_grad.reshape(blocks, DEVICE_POINTS, MODEL_WIDTH)
    slice_wf = w_slice.astype(jnp.float32)

    def front_pass(row_block):
        normed_full, ln_back = jax.vjp(layer_norm, row_block.astype(jnp.float32), ln_gain, ln_bias)
        normed = normed_full.astype(jnp.bfloat16)
        middle = jnp.dot(normed, w_mid, preferred_element_type=jnp.float32).astype(jnp.bfloat16)
        feature = jnp.dot(normed, w_feat, preferred_element_type=jnp.float32).astype(jnp.bfloat16)
        mid_f = middle.astype(jnp.float32).reshape(DEVICE_POINTS, HEADS, HEAD_DIM)
        logits = jnp.einsum('nhd,dm->nhm', mid_f, slice_wf) / temper[None, :, None]
        powers = jnp.exp(logits)
        weights = powers / lax.optimization_barrier(jnp.sum(powers, axis=-1, keepdims=True))
        slice_weight = weights.astype(jnp.bfloat16)
        return (ln_back, normed, middle, feature, logits, weights, slice_weight)

    def gather_step(running_total, block_pair):
        row_block, grad_block = block_pair
        outputs = front_pass(row_block)
        slice_float = outputs[6].astype(jnp.float32)
        feature_float = outputs[3].astype(jnp.float32).reshape(DEVICE_POINTS, HEADS, HEAD_DIM)
        slice_totals = running_total[0] + jnp.einsum('wfr,wfy->fry', slice_float, feature_float)
        masses = running_total[1] + lax.optimization_barrier(jnp.sum(slice_float, axis=0))
        projected_points = running_total[2] + jnp.einsum('nhm,nc->hmc', slice_float, grad_block.astype(jnp.float32))
        return ((slice_totals, masses, projected_points), None)
    start = (jnp.zeros((HEADS, SLICES, HEAD_DIM), jnp.float32), jnp.zeros((HEADS, SLICES), jnp.float32), jnp.zeros((HEADS, SLICES, MODEL_WIDTH), jnp.float32))
    (slice_totals, masses, projected_points), _ = lax.scan(gather_step, start, (point_blocks, grad_blocks))
    slice_tokens = slice_totals / (masses[..., None] + 1e-05)
    mixed, mix_back = jax.vjp(token_mix, slice_tokens, query_weight, key_weight, value_weight)
    mixed_bfloat = mixed.astype(jnp.bfloat16)
    mixed_float = mixed_bfloat.astype(jnp.float32)
    output_per_head = w_out.astype(jnp.float32).reshape(HEADS, HEAD_DIM, MODEL_WIDTH)
    mixed_gradient = jnp.einsum('nov,njv->noj', projected_points, output_per_head, precision=highest_precision)
    output_weight_gradient = jnp.einsum('zgo,zgl->zol', mixed_float, projected_points, precision=highest_precision).reshape(MODEL_WIDTH, MODEL_WIDTH) / TOTAL_POINTS
    d_tokens, grad_query, grad_key, grad_value = mix_back(mixed_gradient)
    masses_gradient = -lax.optimization_barrier(jnp.sum(d_tokens * slice_tokens, axis=-1)) / (masses + 1e-05)
    totals_gradient_float = (d_tokens / (masses[..., None] + 1e-05)).astype(jnp.bfloat16).astype(jnp.float32)

    def backward_step(running_total, block_pair):
        row_block, grad_block = block_pair
        ln_back, normed, middle, feature, logits, weights, slice_weight = front_pass(row_block)
        slice_float = slice_weight.astype(jnp.float32)
        feature_float = feature.astype(jnp.float32).reshape(DEVICE_POINTS, HEADS, HEAD_DIM)
        mid_f = middle.astype(jnp.float32).reshape(DEVICE_POINTS, HEADS, HEAD_DIM)
        d_desliced = jnp.dot(grad_block, w_out.T, preferred_element_type=jnp.float32).astype(jnp.bfloat16)
        desliced_float = d_desliced.astype(jnp.float32).reshape(DEVICE_POINTS, HEADS, HEAD_DIM)
        weights_gradient = jnp.einsum('xbs,bqs->xbq', desliced_float, mixed_float) + jnp.einsum('xbs,bqs->xbq', feature_float, totals_gradient_float) + masses_gradient[None]
        feature_gradient = jnp.einsum('ztl,tlw->ztw', slice_float, totals_gradient_float).astype(jnp.bfloat16).reshape(DEVICE_POINTS, MODEL_WIDTH)
        d_logits = weights * (weights_gradient - lax.optimization_barrier(jnp.sum(weights_gradient * weights, axis=-1, keepdims=True)))
        scaled = (d_logits / temper[None, :, None]).astype(jnp.bfloat16)
        scaled_f = scaled.astype(jnp.float32)
        d_mid = jnp.einsum('nhm,dm->nhd', scaled_f, slice_wf).astype(jnp.bfloat16).reshape(DEVICE_POINTS, MODEL_WIDTH)
        grad_slice = running_total[2] + jnp.einsum('nhd,nhm->dm', mid_f, scaled_f)
        grad_temper = running_total[3] - lax.optimization_barrier(jnp.sum(d_logits * logits, axis=(0, 2))) / temper
        grad_mid = running_total[0] + jnp.dot(normed.T, d_mid, preferred_element_type=jnp.float32)
        grad_feat = running_total[1] + jnp.dot(normed.T, feature_gradient, preferred_element_type=jnp.float32)
        d_normed = jnp.dot(d_mid, w_mid.T, preferred_element_type=jnp.float32) + jnp.dot(feature_gradient, w_feat.T, preferred_element_type=jnp.float32)
        d_values, d_gain, d_bias = ln_back(d_normed)
        updated = (grad_mid, grad_feat, grad_slice, grad_temper, running_total[4] + d_gain, running_total[5] + d_bias)
        return (updated, d_values.astype(jnp.bfloat16))
    start = (jnp.zeros((MODEL_WIDTH, MODEL_WIDTH), jnp.float32), jnp.zeros((MODEL_WIDTH, MODEL_WIDTH), jnp.float32), jnp.zeros((HEAD_DIM, SLICES), jnp.float32), jnp.zeros((HEADS,), jnp.float32), jnp.zeros((MODEL_WIDTH,), jnp.float32), jnp.zeros((MODEL_WIDTH,), jnp.float32))
    sums, point_grads = lax.scan(backward_step, start, (point_blocks, grad_blocks))
    grad_points = point_grads.reshape(TOTAL_POINTS, MODEL_WIDTH)
    return (grad_points, sums[4] / TOTAL_POINTS, sums[5] / TOTAL_POINTS, sums[0] / TOTAL_POINTS, sums[1] / TOTAL_POINTS, sums[2] / TOTAL_POINTS, sums[3] / TOTAL_POINTS, grad_query / TOTAL_POINTS, grad_key / TOTAL_POINTS, grad_value / TOTAL_POINTS, output_weight_gradient)
```

```python
import functools

import jax
import jax.numpy as jnp
from jax import lax
from jax.experimental import pallas as pl
from jax.experimental.pallas import tpu as pltpu
from jax.sharding import PartitionSpec as P

MESH = pl.DeviceIdType.MESH
F32, BF16 = jnp.float32, jnp.bfloat16
HI = lax.Precision.HIGHEST

HEADS, SLICES, DIM = 8, 64, 32
WIDTH = HEADS * DIM
COLS = HEADS * SLICES
NX, NY, NZ, NC = 4, 4, 16, 2
NXY = NX * NY
LOW = 4
NZH = NZ // LOW
PLANE = NXY * LOW
ROWS1, ROWS2 = 9, 13
SMALL = 40
BF_MAX = 3.3895314e38


def dot(a, b, ca=1, cb=0, precision=None):
    return lax.dot_general(
        a, b, (((ca,), (cb,)), ((), ())), preferred_element_type=F32, precision=precision
    )


def iota(shape, dim):
    return lax.broadcasted_iota(jnp.int32, shape, dim)


def split(values):
    high = values.astype(BF16)
    return high, (values - high.astype(F32)).astype(BF16)


def group_sum(high, low, ones):
    parts = []
    for g in range(0, COLS, 256):
        parts.append(dot(high[:, g : g + 256], ones) + dot(low[:, g : g + 256], ones))
    return jnp.concatenate(parts, axis=1)


def block_diagonal(tile_t):
    whole = jnp.concatenate([tile_t] * HEADS, axis=0)
    own = iota((WIDTH, COLS), 0) // DIM == iota((WIDTH, COLS), 1) // SLICES
    return jnp.where(own, whole, 0.0)


def diagonal_rows(full):
    left = iota((DIM, 128), 1) < SLICES
    parts = []
    for g in range(HEADS // 2):
        cols = slice(128 * g, 128 * g + 128)
        parts.append(
            jnp.where(
                left,
                full[2 * DIM * g : 2 * DIM * g + DIM, cols],
                full[2 * DIM * g + DIM : 2 * DIM * g + 2 * DIM, cols],
            )
        )
    return parts


def token_step(totals, masses, d_mixed, wq, wk, wv):
    scale = DIM ** (-0.5)
    inv = 1.0 / (masses + 1e-05)
    tokens = totals * inv
    q = dot(wq, tokens, 0, 0, HI)
    k = dot(wk, tokens, 0, 0, HI)
    v = dot(wv, tokens, 0, 0, HI)
    same = iota((128, 128), 0) // SLICES == iota((128, 128), 1) // SLICES
    mixed, dq, dk, dv = [], [], [], []
    for g in range(HEADS // 2):
        cols = slice(128 * g, 128 * g + 128)
        qg, kg, vg, dmg = q[:, cols], k[:, cols], v[:, cols], d_mixed[:, cols]
        powers = jnp.where(same, jnp.exp(dot(qg, kg, 0, 0, HI) * scale), 0.0)
        att = powers / jnp.sum(powers, axis=1, keepdims=True)
        mixed.append(dot(vg, att, 1, 1, HI))
        dv.append(dot(dmg, att, 1, 0, HI))
        d_att = dot(dmg, vg, 0, 0, HI)
        d_scores = att * (d_att - jnp.sum(d_att * att, axis=1, keepdims=True)) * scale
        dq.append(dot(kg, d_scores, 1, 1, HI))
        dk.append(dot(qg, d_scores, 1, 0, HI))
    join = functools.partial(jnp.concatenate, axis=1)
    mixed, dq, dk, dv = join(mixed), join(dq), join(dk), join(dv)
    d_tokens = dot(wq, dq, 1, 0, HI) + dot(wk, dk, 1, 0, HI) + dot(wv, dv, 1, 0, HI)
    grads = [dot(tokens, d, 1, 1, HI) for d in (dq, dk, dv)]
    d_masses = -jnp.sum(d_tokens * tokens, axis=0, keepdims=True) * inv
    return mixed, d_tokens * inv, d_masses, grads


def kernel(
    everyone,
    chunk,
    points,
    out_grad,
    gain_ref,
    bias_ref,
    w_mid,
    w_feat,
    w_slice,
    temper,
    wq,
    wk,
    wv,
    w_out,
    o_points,
    o_gain,
    o_bias,
    o_mid,
    o_feat,
    o_slice,
    o_temper,
    o_q,
    o_k,
    o_v,
    o_out,
    xhat_s,
    rstd_s,
    normed_s,
    mid_s,
    fd_s,
    low_s,
    logits_s,
    w_s,
    sw_s,
    sc_s,
    dmf_s,
    ds_s,
    p1,
    r10,
    a1,
    r11,
    r12,
    r13,
    p2,
    r20,
    a2,
    r21,
    r22,
    c2,
    r23,
    sends,
    recvs,
):
    p, c = lax.axis_index("pts"), lax.axis_index("rep")
    xy, z = p // NZ, p % NZ
    zl, zh = z % LOW, z // LOW
    rows = points.shape[0]

    def at(xy_, z_, c_):
        return (xy_ * NZ + z_, c_)

    def plane_core(j):
        t = (xy * NC + c + j) % (NXY * NC)
        return at(t // NC, z, t % NC)

    def plane(j):
        return at((xy + j) % NXY, z, c)

    def column(j):
        return at(xy, (z + j) % NZ, c)

    def block(j):
        t = (xy * LOW + zl + j) % PLANE
        return at(t // LOW, zh * LOW + t % LOW, c)

    def block_other(j):
        return at((xy + 1 + j // (LOW - 1)) % NXY, zh * LOW + (zl + 1 + j % (LOW - 1)) % LOW, c)

    def column_high(j):
        return at(xy, (z + LOW * j) % NZ, c)

    sibling = (p, 1 - c)

    barrier = pltpu.get_barrier_semaphore()

    def greet(who, first, last):
        def body(j, _):
            pl.semaphore_signal(barrier, inc=1, device_id=who(j), device_id_type=MESH)
            return 0

        lax.fori_loop(first, last, body, 0)

    n_other = (NXY - 1) * (LOW - 1)
    greet(plane_core, 1, NXY * NC)
    greet(column, 1, NZ)
    greet(block_other, 0, n_other)

    def send_all(stage, who, count, src, dst):
        def body(j, _):
            pltpu.make_async_remote_copy(
                src(j), dst, sends.at[stage], recvs.at[stage], device_id=who(j), device_id_type=MESH
            ).start()
            return 0

        lax.fori_loop(1, count + 1, body, 0)

    def wait_recv(stage, ref):
        pltpu.make_async_remote_copy(
            ref, ref, sends.at[stage], recvs.at[stage], device_id=sibling, device_id_type=MESH
        ).wait_recv()

    def wait_send(stage, ref):
        pltpu.make_async_remote_copy(
            ref, ref, sends.at[stage], recvs.at[stage], device_id=sibling, device_id_type=MESH
        ).wait_send()

    gain, bias = gain_ref[...], bias_ref[...]
    head_of = iota((1, COLS), 1) // SLICES
    temper_row = jnp.zeros((1, COLS), F32)
    for h in range(HEADS):
        temper_row = jnp.where(head_of == h, temper[h], temper_row)
    inv_t = 1.0 / temper_row
    ones = (iota((256, 256), 0) // SLICES == iota((256, 256), 1) // SLICES).astype(F32).astype(BF16)
    ws = w_slice[...].astype(F32)
    slice_blocks = block_diagonal(jnp.concatenate([ws] * HEADS, axis=1)).astype(BF16)

    for r in range(0, rows, chunk):
        here = pl.ds(r, chunk)
        x = points[here, :].astype(F32)
        center = x - jnp.mean(x, axis=1, keepdims=True)
        rstd = lax.rsqrt(jnp.mean(center * center, axis=1, keepdims=True) + 1e-05)
        xhat = center * rstd
        xhat_s[here, :] = xhat
        rstd_s[here, :] = jnp.broadcast_to(rstd, (chunk, 128))
        normed = (xhat * gain + bias).astype(BF16)
        normed_s[here, :] = normed
        mid = dot(normed, w_mid[...]).astype(BF16)
        mid_s[here, :] = mid
        fd_s[here, WIDTH:] = dot(normed, w_feat[...]).astype(BF16)
        logits = dot(mid, slice_blocks) * inv_t
        logits_s[here, :] = logits
        powers = jnp.exp(logits)
        high = jnp.minimum(powers, BF_MAX).astype(BF16)
        low = (powers - high.astype(F32)).astype(BF16)
        weights = powers / group_sum(high, low, ones)
        w_s[here, :] = weights
        sw_s[here, :] = weights.astype(BF16)
        d_high, d_low = split(dot(out_grad[here, :], w_out[...], 1, 1))
        fd_s[here, :WIDTH] = d_high
        low_s[here, :] = d_low

    sw = sw_s[...]
    by_fd = dot(fd_s[...], sw, 0, 0)
    by_low = dot(low_s[...], sw, 0, 0)
    tot = diagonal_rows(by_fd[WIDTH:])
    dmx = diagonal_rows(by_fd[:WIDTH] + by_low)
    mass = dot(jnp.ones((8, rows), BF16), sw)[:1]
    quarter = iota((1, 128), 1) // DIM
    for i in range(4):
        for j in range(4):
            k = 4 * i + j
            p1[0, k, 0:8, :] = tot[j][8 * i : 8 * i + 8]
            p1[1, k, 0:8, :] = dmx[j][8 * i : 8 * i + 8]
            p1[0, k, 8:9, :] = jnp.where(quarter == i, mass[:, 128 * j : 128 * j + 128], 0.0)
            p1[1, k, 8:9, :] = jnp.zeros((1, 128), F32)

    pl.semaphore_wait(barrier, NXY * NC - 1 + NZ - 1 + n_other)

    pltpu.make_async_remote_copy(
        p1.at[1 - c], r10, sends.at[0], recvs.at[0], device_id=sibling, device_id_type=MESH
    ).start()
    wait_recv(0, r10)
    a1[...] = p1[c] + r10[...]
    send_all(1, plane, NXY - 1, lambda j: a1.at[(xy + j) % NXY], r11.at[xy])
    r11[xy] = a1[xy]
    wait_recv(1, r11.at[pl.ds(0, NXY - 1)])
    r12[z] = jnp.sum(r11[...], axis=0)
    send_all(2, column, NZ - 1, lambda j: r12.at[z], r12.at[z])
    wait_recv(2, r12.at[pl.ds(0, NZ - 1)])
    me1 = c * NXY + xy
    r13[me1] = jnp.sum(r12[...], axis=0)
    send_all(3, plane_core, NXY * NC - 1, lambda j: r13.at[me1], r13.at[me1])
    wait_recv(3, r13.at[pl.ds(0, NXY * NC - 1)])

    def whole(half):
        return jnp.concatenate(
            [
                jnp.concatenate([r13[NXY * half + 4 * i + j, 0:8, :] for i in range(4)], axis=0)
                for j in range(4)
            ],
            axis=1,
        )

    masses = jnp.concatenate(
        [sum(r13[4 * i + j, 8:9, :] for i in range(4)) for j in range(4)], axis=1
    )
    mixed, d_totals, d_masses, grads = token_step(
        whole(0), masses, whole(1), wq[...], wk[...], wv[...]
    )
    for out, grad in zip((o_q, o_k, o_v), grads):
        out[...] = grad / everyone
    both = jnp.concatenate(
        [
            block_diagonal(mixed.astype(BF16).astype(F32)).astype(BF16),
            block_diagonal(d_totals.astype(BF16).astype(F32)).astype(BF16),
        ],
        axis=0,
    )
    w_both = jnp.concatenate([w_mid[...], w_feat[...]], axis=1)

    temper_sum = jnp.zeros((8, COLS), F32)
    gain_sum = jnp.zeros((8, WIDTH), F32)
    bias_sum = jnp.zeros((8, WIDTH), F32)

    def fold(values):
        return jnp.sum(values.reshape(values.shape[0] // 8, 8, values.shape[1]), axis=0)

    for r in range(0, rows, chunk):
        here = pl.ds(r, chunk)
        weights = w_s[here, :]
        d_weights = dot(fd_s[here, :], both) + d_masses
        high, low = split(d_weights * weights)
        d_logits = weights * (d_weights - group_sum(high, low, ones))
        scaled = (d_logits * inv_t).astype(BF16)
        sc_s[here, :] = scaled
        temper_sum += fold(d_logits * logits_s[here, :])
        d_mid = dot(scaled, slice_blocks, 1, 1).astype(BF16)
        by_both = dot(sw_s[here, :], both, 1, 1)
        d_feat = by_both[:, WIDTH:].astype(BF16)
        s_high, s_low = split(by_both[:, :WIDTH])
        ds_s[here, :WIDTH] = s_high
        ds_s[here, WIDTH:] = s_low
        dmf_s[here, :WIDTH] = d_mid
        dmf_s[here, WIDTH:] = d_feat
        d_normed = dot(dmf_s[here, :], w_both, 1, 1)
        xhat = xhat_s[here, :]
        gain_sum += fold(d_normed * xhat)
        bias_sum += fold(d_normed)
        d_xhat = d_normed * gain
        inner = d_xhat - jnp.mean(d_xhat, axis=1, keepdims=True)
        inner = inner - xhat * jnp.mean(d_xhat * xhat, axis=1, keepdims=True)
        o_points[here, :] = (inner * rstd_s[here, 0:1]).astype(BF16)

    by_normed = dot(normed_s[...], dmf_s[...], 0, 0)
    by_slices = dot(ds_s[...], out_grad[...], 0, 0)
    out_w = by_slices[:WIDTH] + by_slices[WIDTH:]
    slice_sum = sum(diagonal_rows(dot(mid_s[...], sc_s[...], 0, 0)))
    small = jnp.concatenate(
        [jnp.sum(gain_sum, axis=0, keepdims=True)[:, 128 * l : 128 * l + 128] for l in range(2)]
        + [jnp.sum(bias_sum, axis=0, keepdims=True)[:, 128 * l : 128 * l + 128] for l in range(2)]
        + [jnp.sum(temper_sum, axis=0, keepdims=True)[:, 128 * l : 128 * l + 128] for l in range(4)]
        + [slice_sum],
        axis=0,
    )
    for h in range(NC):
        half = slice(128 * h, 128 * h + 128)
        for a in range(2):
            for l in range(2):
                first = WIDTH * a + 128 * l
                p2[h, 32 * a + 16 * l : 32 * a + 16 * l + 16, 0:8, :] = by_normed[
                    half, first : first + 128
                ].reshape(16, 8, 128)
        for l in range(2):
            for s in range(32):
                p2[h, 32 * l + s, 8:12, :] = out_w[
                    128 * h + 4 * s : 128 * h + 4 * s + 4, 128 * l : 128 * l + 128
                ]
        for k in range(PLANE):
            p2[h, k, 12:13, :] = small[k : k + 1] if k < SMALL else jnp.zeros((1, 128), F32)

    pltpu.make_async_remote_copy(
        p2.at[1 - c], r20, sends.at[4], recvs.at[4], device_id=sibling, device_id_type=MESH
    ).start()
    wait_recv(4, r20)
    a2[...] = p2[c] + r20[...]
    t = xy * LOW + zl
    send_all(5, block, PLANE - 1, lambda j: a2.at[(t + j) % PLANE], r21.at[t])
    r21[t] = a2[t]
    wait_recv(5, r21.at[pl.ds(0, PLANE - 1)])
    r22[zh] = jnp.sum(r21[...], axis=0)
    send_all(6, column_high, NZH - 1, lambda j: r22.at[zh], r22.at[zh])
    wait_recv(6, r22.at[pl.ds(0, NZH - 1)])
    r23[t] = jnp.sum(r22[...], axis=0) / everyone
    send_all(7, block, PLANE - 1, lambda j: r23.at[t], r23.at[t])
    wait_recv(7, r23.at[pl.ds(0, PLANE - 1)])

    for a, out in enumerate((o_mid, o_feat)):
        for l in range(2):
            first = 32 * a + 16 * l
            out[:, 128 * l : 128 * l + 128] = r23[first : first + 16, 0:8, :].reshape(128, 128)
    for l in range(2):
        for s in range(32):
            o_out[4 * s : 4 * s + 4, 128 * l : 128 * l + 128] = r23[32 * l + s, 8:12, :]
    for l in range(2):
        o_gain[:, 128 * l : 128 * l + 128] = r23[l, 12:13, :]
        o_bias[:, 128 * l : 128 * l + 128] = r23[2 + l, 12:13, :]
    lane = iota((1, 128), 1)
    d_temper = jnp.zeros((1, 128), F32)
    for g in range(4):
        row = r23[4 + g, 12:13, :]
        for s in range(2):
            part = jnp.sum(jnp.where(lane // SLICES == s, row, 0.0), axis=1, keepdims=True)
            d_temper = jnp.where(lane == 2 * g + s, -part / temper[2 * g + s], d_temper)
    o_temper[...] = d_temper
    folded = jnp.concatenate([r23[8 + d, 12:13, :] for d in range(DIM)], axis=0)
    o_slice[...] = (folded + pltpu.roll(folded, SLICES, 1))[:, :SLICES]

    wait_send(0, r10)
    wait_send(1, r11.at[pl.ds(0, NXY - 1)])
    wait_send(2, r12.at[pl.ds(0, NZ - 1)])
    wait_send(3, r13.at[pl.ds(0, NXY * NC - 1)])
    wait_send(4, r20)
    wait_send(5, r21.at[pl.ds(0, PLANE - 1)])
    wait_send(6, r22.at[pl.ds(0, NZH - 1)])
    wait_send(7, r23.at[pl.ds(0, PLANE - 1)])


def shards(
    points, out_grad, ln_gain, ln_bias, w_mid, w_feat, w_slice, temper, wq, wk, wv, w_out
):
    rows = points.shape[0]
    everyone = rows * NXY * NZ * NC
    vmem = pl.BlockSpec(memory_space=pltpu.VMEM)
    smem = pl.BlockSpec(memory_space=pltpu.SMEM)
    f = lambda *s: jax.ShapeDtypeStruct(s, F32)
    outs = pl.pallas_call(
        functools.partial(kernel, float(everyone), 128),
        out_shape=(
            jax.ShapeDtypeStruct((rows, WIDTH), BF16),
            f(1, WIDTH),
            f(1, WIDTH),
            f(128, WIDTH),
            f(128, WIDTH),
            f(DIM, SLICES),
            f(1, 128),
            f(DIM, DIM),
            f(DIM, DIM),
            f(DIM, DIM),
            f(128, WIDTH),
        ),
        in_specs=[vmem] * 7 + [smem] + [vmem] * 4,
        out_specs=(vmem,) * 11,
        scratch_shapes=[
            pltpu.VMEM((rows, WIDTH), F32),
            pltpu.VMEM((rows, 128), F32),
            pltpu.VMEM((rows, WIDTH), BF16),
            pltpu.VMEM((rows, WIDTH), BF16),
            pltpu.VMEM((rows, 2 * WIDTH), BF16),
            pltpu.VMEM((rows, WIDTH), BF16),
            pltpu.VMEM((rows, COLS), F32),
            pltpu.VMEM((rows, COLS), F32),
            pltpu.VMEM((rows, COLS), BF16),
            pltpu.VMEM((rows, COLS), BF16),
            pltpu.VMEM((rows, 2 * WIDTH), BF16),
            pltpu.VMEM((rows, 2 * WIDTH), BF16),
            pltpu.VMEM((NC, NXY, ROWS1, 128), F32),
            pltpu.VMEM((NXY, ROWS1, 128), F32),
            pltpu.VMEM((NXY, ROWS1, 128), F32),
            pltpu.VMEM((NXY, ROWS1, 128), F32),
            pltpu.VMEM((NZ, ROWS1, 128), F32),
            pltpu.VMEM((NC * NXY, ROWS1, 128), F32),
            pltpu.VMEM((NC, PLANE, ROWS2, 128), F32),
            pltpu.VMEM((PLANE, ROWS2, 128), F32),
            pltpu.VMEM((PLANE, ROWS2, 128), F32),
            pltpu.VMEM((PLANE, ROWS2, 128), F32),
            pltpu.VMEM((NZH, ROWS2, 128), F32),
            pltpu.VMEM((8, 128), F32),
            pltpu.VMEM((PLANE, ROWS2, 128), F32),
            pltpu.SemaphoreType.DMA((8,)),
            pltpu.SemaphoreType.DMA((8,)),
        ],
        compiler_params=pltpu.CompilerParams(
            collective_id=0, has_side_effects=True, vmem_limit_bytes=48 * 1024 * 1024
        ),
    )(
        points,
        out_grad,
        ln_gain.reshape(1, -1),
        ln_bias.reshape(1, -1),
        w_mid,
        w_feat,
        w_slice,
        temper,
        wq,
        wk,
        wv,
        w_out,
    )
    outs = list(outs)
    outs[1] = outs[1].reshape(-1)
    outs[2] = outs[2].reshape(-1)
    outs[6] = outs[6][0, :HEADS]
    return tuple(outs)


def solution(mesh):
    by_point, by_rep = P(("pts", "rep"), None), P("rep", None)
    in_specs = (by_point, by_point) + (P(),) * 10
    out_specs = (by_point, P(), P(), by_rep, by_rep, P(), P(), P(), P(), P(), by_rep)
    return jax.shard_map(shards, mesh=mesh, in_specs=in_specs, out_specs=out_specs, check_vma=False)
```

```python
import functools

import jax
import jax.numpy as jnp
from jax import lax
from jax.experimental import pallas as pl
from jax.experimental.pallas import tpu as pltpu
from jax.sharding import PartitionSpec as P

MESH = pl.DeviceIdType.MESH
F32, BF16 = jnp.float32, jnp.bfloat16
HI = lax.Precision.HIGHEST

HEADS, SLICES, DIM = 8, 64, 32
WIDTH = HEADS * DIM
COLS = HEADS * SLICES
NX, NY, NZ, NC = 4, 4, 16, 2
NXY = NX * NY
LOW = 4
NZH = NZ // LOW
ROWS1, ROWS2 = 9, 19
SMALL = 40
VMEM_BYTES = 60 * 1024 * 1024
BF_MAX = 3.3895314e38


def dot(a, b, ca=1, cb=0, precision=None):
    return lax.dot_general(
        a, b, (((ca,), (cb,)), ((), ())), preferred_element_type=F32, precision=precision
    )


def iota(shape, dim):
    return lax.broadcasted_iota(jnp.int32, shape, dim)


def split(values):
    high = values.astype(BF16)
    return high, (values - high.astype(F32)).astype(BF16)


def group_sum(high, low, ones):
    parts = []
    for g in range(0, COLS, 256):
        parts.append(dot(high[:, g : g + 256], ones) + dot(low[:, g : g + 256], ones))
    return jnp.concatenate(parts, axis=1)


def block_diagonal(tile_t):
    whole = jnp.concatenate([tile_t] * HEADS, axis=0)
    own = iota((WIDTH, COLS), 0) // DIM == iota((WIDTH, COLS), 1) // SLICES
    return jnp.where(own, whole, 0.0)


def diagonal_rows(full):
    left = iota((DIM, 128), 1) < SLICES
    parts = []
    for g in range(HEADS // 2):
        cols = slice(128 * g, 128 * g + 128)
        parts.append(
            jnp.where(
                left,
                full[2 * DIM * g : 2 * DIM * g + DIM, cols],
                full[2 * DIM * g + DIM : 2 * DIM * g + 2 * DIM, cols],
            )
        )
    return parts


def token_step(totals, masses, d_mixed, wq, wk, wv):
    scale = DIM ** (-0.5)
    inv = 1.0 / (masses + 1e-05)
    tokens = totals * inv
    q = dot(wq, tokens, 0, 0, HI)
    k = dot(wk, tokens, 0, 0, HI)
    v = dot(wv, tokens, 0, 0, HI)
    same = iota((128, 128), 0) // SLICES == iota((128, 128), 1) // SLICES
    mixed, dq, dk, dv = [], [], [], []
    for g in range(HEADS // 2):
        cols = slice(128 * g, 128 * g + 128)
        qg, kg, vg, dmg = q[:, cols], k[:, cols], v[:, cols], d_mixed[:, cols]
        powers = jnp.where(same, jnp.exp(dot(qg, kg, 0, 0, HI) * scale), 0.0)
        att = powers / jnp.sum(powers, axis=1, keepdims=True)
        mixed.append(dot(vg, att, 1, 1, HI))
        dv.append(dot(dmg, att, 1, 0, HI))
        d_att = dot(dmg, vg, 0, 0, HI)
        d_scores = att * (d_att - jnp.sum(d_att * att, axis=1, keepdims=True)) * scale
        dq.append(dot(kg, d_scores, 1, 1, HI))
        dk.append(dot(qg, d_scores, 1, 0, HI))
    join = functools.partial(jnp.concatenate, axis=1)
    mixed, dq, dk, dv = join(mixed), join(dq), join(dk), join(dv)
    d_tokens = dot(wq, dq, 1, 0, HI) + dot(wk, dk, 1, 0, HI) + dot(wv, dv, 1, 0, HI)
    grads = [dot(tokens, d, 1, 1, HI) for d in (dq, dk, dv)]
    d_masses = -jnp.sum(d_tokens * tokens, axis=0, keepdims=True) * inv
    return mixed, d_tokens * inv, d_masses, grads


def far_first(a):
    return (2 - a + 3 * (a // 2) - 2 * (a // 3)) % 4


def kernel(
    everyone,
    chunk,
    points_h,
    out_grad_h,
    gain_h,
    bias_h,
    w_mid_h,
    w_feat_h,
    w_slice_h,
    temper_h,
    wq_h,
    wk_h,
    wv_h,
    w_out_h,
    h_points,
    h_gain,
    h_bias,
    h_mid,
    h_feat,
    h_slice,
    h_temper,
    h_q,
    h_k,
    h_v,
    h_out,
    o_points,
    o_gain,
    o_bias,
    o_mid,
    o_feat,
    o_slice,
    o_temper,
    o_q,
    o_k,
    o_v,
    o_out,
    stores,
    points,
    out_grad,
    gain_ref,
    bias_ref,
    w_mid,
    w_feat,
    w_slice,
    temper,
    wq,
    wk,
    wv,
    w_out,
    loads,
    xhat_s,
    rstd_s,
    normed_s,
    mid_s,
    fd_s,
    low_s,
    logits_s,
    w_s,
    sw_s,
    sc_s,
    dmf_s,
    ds_s,
    dn_s,
    p1,
    r10,
    a1,
    r11,
    r12,
    r13,
    pa,
    ra0,
    aa,
    ra1,
    ra2,
    ra3,
    ra4,
    ra5,
    pb,
    rb0,
    ab,
    rb1,
    rb2,
    rb3,
    sends,
    recvs,
):
    held = (
        (points_h, points),
        (w_mid_h, w_mid),
        (w_feat_h, w_feat),
        (gain_h, gain_ref),
        (bias_h, bias_ref),
        (w_slice_h, w_slice),
        (temper_h, temper),
        (out_grad_h, out_grad),
        (w_out_h, w_out),
        (wq_h, wq),
        (wk_h, wk),
        (wv_h, wv),
    )
    copies = [pltpu.make_async_copy(a, b, loads.at[n]) for n, (a, b) in enumerate(held)]
    for copy in copies:
        copy.start()

    p, c = lax.axis_index("pts"), lax.axis_index("rep")
    x, y, z = p // (NY * NZ), p // NZ % NY, p % NZ
    xy = x * NY + y
    zl, zh = z % LOW, z // LOW
    rows = points.shape[0]

    def plane_index(i):
        return (x + far_first(i // 4)) % NX * NY + (y + far_first(i % 4)) % NY

    def plane(i):
        return (plane_index(i) * NZ + z, c)

    def plane_cores(i):
        return (plane_index(i // 2) * NZ + z, (c + 1 + i % 2) % NC)

    def column(i):
        return (xy * NZ + (z + 8 + (i + 1) // 2 * (1 - 2 * (i % 2))) % NZ, c)

    def low_index(i):
        return (zl + far_first(i)) % LOW

    def column_low(i):
        return (xy * NZ + zh * LOW + low_index(i), c)

    def column_high(i):
        return (xy * NZ + (z + LOW * far_first(i)) % NZ, c)

    sibling = (p, 1 - c)
    made = (
        (o_points, h_points),
        (o_gain, h_gain),
        (o_bias, h_bias),
        (o_mid, h_mid),
        (o_feat, h_feat),
        (o_slice, h_slice),
        (o_temper, h_temper),
        (o_q, h_q),
        (o_k, h_k),
        (o_v, h_v),
        (o_out, h_out),
    )
    writes = [pltpu.make_async_copy(a, b, stores.at[n]) for n, (a, b) in enumerate(made)]

    barrier = pltpu.get_barrier_semaphore()

    def greet(who, count):
        def body(i, _):
            pl.semaphore_signal(barrier, inc=1, device_id=who(i), device_id_type=MESH)
            return 0

        lax.fori_loop(0, count, body, 0)

    with jax.named_scope("greet"):
        greet(plane_cores, 2 * NXY - 1)
        greet(column, NZ - 1)

    unsent, started = [], []

    def send_all(stage, who, count, src, dst):
        def body(i, _):
            pltpu.make_async_remote_copy(
                src(i), dst, sends.at[stage], recvs.at[stage], device_id=who(i), device_id_type=MESH
            ).start()
            return 0

        lax.fori_loop(0, count, body, 0)

    def swap(stage, src, dst):
        send_all(stage, lambda i: sibling, 1, lambda i: src, dst)

    def wait(stage, ref):
        copy = pltpu.make_async_remote_copy(
            ref, ref, sends.at[stage], recvs.at[stage], device_id=sibling, device_id_type=MESH
        )
        copy.wait_recv()
        unsent.append(copy)

    def write(n):
        writes[n].start()
        started.append(writes[n])

    ones = (iota((256, 256), 0) // SLICES == iota((256, 256), 1) // SLICES).astype(F32).astype(BF16)

    with jax.named_scope("load"):
        for copy in copies:
            copy.wait()
    gain, bias = gain_ref[...], bias_ref[...]
    head_of = iota((1, COLS), 1) // SLICES
    temper_row = jnp.zeros((1, COLS), F32)
    for h in range(HEADS):
        temper_row = jnp.where(head_of == h, temper[:, h : h + 1], temper_row)
    inv_t = 1.0 / temper_row
    ws = w_slice[...].astype(F32)
    slice_blocks = block_diagonal(jnp.concatenate([ws] * HEADS, axis=1)).astype(BF16)

    with jax.named_scope("front"):
        for r in range(0, rows, chunk):
            here = pl.ds(r, chunk)
            xs = points[here, :].astype(F32)
            center = xs - jnp.mean(xs, axis=1, keepdims=True)
            rstd = lax.rsqrt(jnp.mean(center * center, axis=1, keepdims=True) + 1e-05)
            xhat = center * rstd
            xhat_s[here, :] = xhat
            rstd_s[here, :] = jnp.broadcast_to(rstd, (chunk, 128))
            normed = (xhat * gain + bias).astype(BF16)
            normed_s[here, :] = normed
            mid = dot(normed, w_mid[...]).astype(BF16)
            mid_s[here, :] = mid
            fd_s[here, WIDTH:] = dot(normed, w_feat[...]).astype(BF16)
            logits = dot(mid, slice_blocks) * inv_t
            logits_s[here, :] = logits
            powers = jnp.exp(logits)
            high = jnp.minimum(powers, BF_MAX).astype(BF16)
            low = (powers - high.astype(F32)).astype(BF16)
            weights = powers / group_sum(high, low, ones)
            w_s[here, :] = weights
            sw_s[here, :] = weights.astype(BF16)
            d_high, d_low = split(dot(out_grad[here, :], w_out[...], 1, 1))
            fd_s[here, :WIDTH] = d_high
            low_s[here, :] = d_low

    with jax.named_scope("shares1"):
        sw = sw_s[...]
        by_fd = dot(fd_s[...], sw, 0, 0)
        by_low = dot(low_s[...], sw, 0, 0)
        tot = diagonal_rows(by_fd[WIDTH:])
        dmx = diagonal_rows(by_fd[:WIDTH] + by_low)
        mass = dot(jnp.ones((8, rows), BF16), sw)[:1]
        quarter = iota((1, 128), 1) // DIM
        for i in range(4):
            for j in range(4):
                k = 4 * i + j
                p1[0, k, 0:8, :] = tot[j][8 * i : 8 * i + 8]
                p1[1, k, 0:8, :] = dmx[j][8 * i : 8 * i + 8]
                p1[0, k, 8:9, :] = jnp.where(quarter == i, mass[:, 128 * j : 128 * j + 128], 0.0)
                p1[1, k, 8:9, :] = jnp.zeros((1, 128), F32)

    with jax.named_scope("barrier"):
        pl.semaphore_wait(barrier, 2 * NXY - 1 + NZ - 1)

    with jax.named_scope("sum1_core"):
        swap(0, p1.at[1 - c], r10)
        wait(0, r10)
        a1[...] = p1[c] + r10[...]
    with jax.named_scope("sum1_plane"):
        send_all(1, plane, NXY - 1, lambda i: a1.at[plane_index(i)], r11.at[xy])
        r11[xy] = a1[xy]
        wait(1, r11.at[pl.ds(0, NXY - 1)])
        r12[z] = jnp.sum(r11[...], axis=0)
    with jax.named_scope("sum1_column"):
        send_all(2, column, NZ - 1, lambda i: r12.at[z], r12.at[z])
        wait(2, r12.at[pl.ds(0, NZ - 1)])
        me1 = c * NXY + xy
        r13[me1] = jnp.sum(r12[...], axis=0)
    with jax.named_scope("sum1_back"):
        send_all(3, plane_cores, 2 * NXY - 1, lambda i: r13.at[me1], r13.at[me1])
        wait(3, r13.at[pl.ds(0, 2 * NXY - 1)])

    def whole(half):
        return jnp.concatenate(
            [
                jnp.concatenate([r13[NXY * half + 4 * i + j, 0:8, :] for i in range(4)], axis=0)
                for j in range(4)
            ],
            axis=1,
        )

    with jax.named_scope("tokens"):
        masses = jnp.concatenate(
            [sum(r13[4 * i + j, 8:9, :] for i in range(4)) for j in range(4)], axis=1
        )
        mixed, d_totals, d_masses, grads = token_step(
            whole(0), masses, whole(1), wq[...], wk[...], wv[...]
        )
        for out, grad in zip((o_q, o_k, o_v), grads):
            out[...] = grad / everyone
        for n in (7, 8, 9):
            write(n)
        both = jnp.concatenate(
            [
                block_diagonal(mixed.astype(BF16).astype(F32)).astype(BF16),
                block_diagonal(d_totals.astype(BF16).astype(F32)).astype(BF16),
            ],
            axis=0,
        )

    with jax.named_scope("feat_out"):
        for r in range(0, rows, chunk):
            here = pl.ds(r, chunk)
            by_both = dot(sw_s[here, :], both, 1, 1)
            dmf_s[here, WIDTH:] = by_both[:, WIDTH:].astype(BF16)
            s_high, s_low = split(by_both[:, :WIDTH])
            ds_s[here, :WIDTH] = s_high
            ds_s[here, WIDTH:] = s_low
        by_normed = dot(normed_s[...], dmf_s[:, WIDTH:], 0, 0)
        by_slices = dot(ds_s[...], out_grad[...], 0, 0)
        out_w = by_slices[:WIDTH] + by_slices[WIDTH:]
        for h in range(NC):
            half = slice(128 * h, 128 * h + 128)
            for a, grad in enumerate((by_normed, out_w)):
                for l in range(2):
                    first = 8 * a + 4 * l
                    pa[h, first : first + 4] = grad[half, 128 * l : 128 * l + 128].reshape(
                        4, LOW, 8, 128
                    )
        swap(4, pa.at[1 - c], ra0)

    w_both = jnp.concatenate([w_mid[...], w_feat[...]], axis=1)

    def fold(values):
        return jnp.sum(values.reshape(values.shape[0] // 8, 8, values.shape[1]), axis=0)

    sums = [jnp.zeros((8, COLS), F32), jnp.zeros((8, WIDTH), F32), jnp.zeros((8, WIDTH), F32)]

    def back(r):
        here = pl.ds(r, chunk)
        weights = w_s[here, :]
        d_weights = dot(fd_s[here, :], both) + d_masses
        high, low = split(d_weights * weights)
        d_logits = weights * (d_weights - group_sum(high, low, ones))
        scaled = (d_logits * inv_t).astype(BF16)
        sc_s[here, :] = scaled
        sums[0] += fold(d_logits * logits_s[here, :])
        dmf_s[here, :WIDTH] = dot(scaled, slice_blocks, 1, 1).astype(BF16)
        d_normed = dot(dmf_s[here, :], w_both, 1, 1)
        dn_s[here, :] = d_normed
        sums[1] += fold(d_normed * xhat_s[here, :])
        sums[2] += fold(d_normed)

    with jax.named_scope("back_first"):
        for r in range(0, rows // 2, chunk):
            back(r)
    with jax.named_scope("suma_core"):
        wait(4, ra0)
        aa[...] = pa[c] + ra0[...]
        send_all(5, plane, NXY - 1, lambda i: aa.at[plane_index(i)], ra1.at[xy])
        ra1[xy] = aa[xy]
    with jax.named_scope("back_second"):
        for r in range(rows // 2, rows, chunk):
            back(r)
    with jax.named_scope("sharesb"):
        grad_mid = dot(normed_s[...], dmf_s[:, :WIDTH], 0, 0)
        slice_sum = sum(diagonal_rows(dot(mid_s[...], sc_s[...], 0, 0)))
        temper_sum, gain_sum, bias_sum = (jnp.sum(v, axis=0, keepdims=True) for v in sums)
        small = [gain_sum[:, 128 * l : 128 * l + 128] for l in range(2)]
        small += [bias_sum[:, 128 * l : 128 * l + 128] for l in range(2)]
        small += [temper_sum[:, 128 * l : 128 * l + 128] for l in range(4)]
        small += [slice_sum[d : d + 1] for d in range(DIM)]
        small += [jnp.zeros((1, 128), F32)] * (3 * NXY - len(small))
        small = jnp.concatenate(small, axis=0)
        for h in range(NC):
            for l in range(2):
                pb[h, 8 * l : 8 * l + 8, 0:16, :] = grad_mid[
                    128 * h : 128 * h + 128, 128 * l : 128 * l + 128
                ].reshape(8, 16, 128)
            for k in range(NXY):
                pb[h, k, 16:19, :] = small[3 * k : 3 * k + 3]

    with jax.named_scope("sumb_core"):
        swap(9, pb.at[1 - c], rb0)
    with jax.named_scope("suma_plane"):
        wait(5, ra1.at[pl.ds(0, NXY - 1)])
        ra2[...] = jnp.sum(ra1[...], axis=0)
        send_all(6, column_low, LOW - 1, lambda i: ra2.at[low_index(i)], ra3.at[zl])
        ra3[zl] = ra2[zl]
    with jax.named_scope("sumb_plane"):
        wait(9, rb0)
        ab[...] = pb[c] + rb0[...]
        send_all(10, plane, NXY - 1, lambda i: ab.at[plane_index(i)], rb1.at[xy])
        rb1[xy] = ab[xy]

    with jax.named_scope("points"):
        for r in range(0, rows, chunk):
            here = pl.ds(r, chunk)
            xhat = xhat_s[here, :]
            d_xhat = dn_s[here, :] * gain
            inner = d_xhat - jnp.mean(d_xhat, axis=1, keepdims=True)
            inner = inner - xhat * jnp.mean(d_xhat * xhat, axis=1, keepdims=True)
            o_points[here, :] = (inner * rstd_s[here, 0:1]).astype(BF16)
        write(0)

    with jax.named_scope("suma_low"):
        wait(6, ra3.at[pl.ds(0, LOW - 1)])
        ra4[zh] = jnp.sum(ra3[...], axis=0)
        send_all(7, column_high, NZH - 1, lambda i: ra4.at[zh], ra4.at[zh])
    with jax.named_scope("sumb_column"):
        wait(10, rb1.at[pl.ds(0, NXY - 1)])
        rb2[z] = jnp.sum(rb1[...], axis=0)
        send_all(11, column, NZ - 1, lambda i: rb2.at[z], rb2.at[z])
    with jax.named_scope("suma_high"):
        wait(7, ra4.at[pl.ds(0, NZH - 1)])
        ra5[xy, zl] = jnp.sum(ra4[...], axis=0) / everyone
        send_all(8, column_low, LOW - 1, lambda i: ra5.at[xy, zl], ra5.at[xy, zl])
        wait(8, ra5.at[xy, pl.ds(0, LOW - 1)])
        send_all(12, plane, NXY - 1, lambda i: ra5.at[xy], ra5.at[xy])
    with jax.named_scope("sumb_back"):
        wait(11, rb2.at[pl.ds(0, NZ - 1)])
        rb3[xy] = jnp.sum(rb2[...], axis=0) / everyone
        send_all(13, plane, NXY - 1, lambda i: rb3.at[xy], rb3.at[xy])
    with jax.named_scope("suma_last"):
        wait(12, ra5.at[pl.ds(0, NXY - 1)])
        for a, out in enumerate((o_feat, o_out)):
            for l in range(2):
                first = 8 * a + 4 * l
                out[:, 128 * l : 128 * l + 128] = ra5[first : first + 4].reshape(128, 128)
        write(4)
        write(10)
    with jax.named_scope("sumb_last"):
        wait(13, rb3.at[pl.ds(0, NXY - 1)])
        for l in range(2):
            o_mid[:, 128 * l : 128 * l + 128] = rb3[8 * l : 8 * l + 8, 0:16, :].reshape(128, 128)
        small = [rb3[k // 3, 16 + k % 3 : 17 + k % 3, :] for k in range(SMALL)]
        for l in range(2):
            o_gain[:, 128 * l : 128 * l + 128] = small[l]
            o_bias[:, 128 * l : 128 * l + 128] = small[2 + l]
        folded = jnp.concatenate(small[8:], axis=0)
        o_slice[...] = (folded + pltpu.roll(folded, SLICES, 1))[:, :SLICES]
        lane, place = iota((1, 128), 1), iota((1, HEADS), 1)
        d_temper = jnp.zeros((1, HEADS), F32)
        for g in range(4):
            for s in range(2):
                part = jnp.where(lane // SLICES == s, small[4 + g], 0.0)
                part = jnp.sum(part, axis=1, keepdims=True)
                d_temper = jnp.where(place == 2 * g + s, part, d_temper)
        o_temper[...] = -d_temper / temper[...]
        for n in (1, 2, 3, 5, 6):
            write(n)

    with jax.named_scope("done"):
        for copy in unsent:
            copy.wait_send()
        for copy in started:
            copy.wait()


def hand_on(count, *refs):
    ins, outs, held, (loads, stores) = (
        refs[:count],
        refs[count : 2 * count],
        refs[2 * count : 3 * count],
        refs[3 * count :],
    )
    one = [pltpu.make_async_copy(ins[n], held[n], loads.at[n]) for n in range(count)]
    two = [pltpu.make_async_copy(held[n], outs[n], stores.at[n]) for n in range(count)]
    for copy in one:
        copy.start()
    for first, second in zip(one, two):
        first.wait()
        second.start()
    for copy in two:
        copy.wait()


def shards(
    points, out_grad, ln_gain, ln_bias, w_mid, w_feat, w_slice, temper, wq, wk, wv, w_out
):
    rows = points.shape[0]
    everyone = rows * NXY * NZ * NC
    hbm = pl.BlockSpec(memory_space=pltpu.HBM)
    f = lambda *s: jax.ShapeDtypeStruct(s, F32)
    args = (
        points,
        out_grad,
        ln_gain.reshape(1, -1),
        ln_bias.reshape(1, -1),
        w_mid,
        w_feat,
        w_slice,
        temper.reshape(1, -1),
        wq,
        wk,
        wv,
        w_out,
    )
    out_shape = (
        jax.ShapeDtypeStruct((rows, WIDTH), BF16),
        f(1, WIDTH),
        f(1, WIDTH),
        f(128, WIDTH),
        f(128, WIDTH),
        f(DIM, SLICES),
        f(1, HEADS),
        f(DIM, DIM),
        f(DIM, DIM),
        f(DIM, DIM),
        f(128, WIDTH),
    )
    outs = pl.pallas_call(
        functools.partial(kernel, float(everyone), 128),
        out_shape=out_shape,
        in_specs=[hbm] * 12,
        out_specs=(hbm,) * 11,
        scratch_shapes=[pltpu.VMEM(a.shape, a.dtype) for a in out_shape]
        + [pltpu.SemaphoreType.DMA((11,))]
        + [pltpu.VMEM(a.shape, a.dtype) for a in args]
        + [pltpu.SemaphoreType.DMA((12,))]
        + [
            pltpu.VMEM((rows, WIDTH), F32),
            pltpu.VMEM((rows, 128), F32),
            pltpu.VMEM((rows, WIDTH), BF16),
            pltpu.VMEM((rows, WIDTH), BF16),
            pltpu.VMEM((rows, 2 * WIDTH), BF16),
            pltpu.VMEM((rows, WIDTH), BF16),
            pltpu.VMEM((rows, COLS), F32),
            pltpu.VMEM((rows, COLS), F32),
            pltpu.VMEM((rows, COLS), BF16),
            pltpu.VMEM((rows, COLS), BF16),
            pltpu.VMEM((rows, 2 * WIDTH), BF16),
            pltpu.VMEM((rows, 2 * WIDTH), BF16),
            pltpu.VMEM((rows, WIDTH), F32),
        ]
        + [
            pltpu.VMEM(lead + (ROWS1, 128), F32)
            for lead in ((NC, NXY), (NXY,), (NXY,), (NXY,), (NZ,), (NC * NXY,))
        ]
        + [
            pltpu.VMEM(lead + (8, 128), F32)
            for lead in (
                (NC, NXY, LOW),
                (NXY, LOW),
                (NXY, LOW),
                (NXY, LOW),
                (LOW,),
                (LOW,),
                (NZH,),
                (NXY, LOW),
            )
        ]
        + [
            pltpu.VMEM(lead + (ROWS2, 128), F32)
            for lead in ((NC, NXY), (NXY,), (NXY,), (NXY,), (NZ,), (NXY,))
        ]
        + [pltpu.SemaphoreType.DMA((14,)), pltpu.SemaphoreType.DMA((14,))],
        compiler_params=pltpu.CompilerParams(
            collective_id=0, has_side_effects=True, vmem_limit_bytes=VMEM_BYTES
        ),
        name="backward",
    )(*args)
    outs = pl.pallas_call(
        functools.partial(hand_on, len(outs)),
        out_shape=out_shape,
        in_specs=[hbm] * 11,
        out_specs=(hbm,) * 11,
        scratch_shapes=[pltpu.VMEM(a.shape, a.dtype) for a in out_shape]
        + [pltpu.SemaphoreType.DMA((11,))] * 2,
        compiler_params=pltpu.CompilerParams(vmem_limit_bytes=VMEM_BYTES),
        name="hand_on",
    )(*outs)
    outs = list(outs)
    for n in (1, 2, 6):
        outs[n] = outs[n].reshape(-1)
    return tuple(outs)


def solution(mesh):
    by_point, by_rep = P(("pts", "rep"), None), P("rep", None)
    in_specs = (by_point, by_point) + (P(),) * 10
    out_specs = (by_point, P(), P(), by_rep, by_rep, P(), P(), P(), P(), P(), by_rep)
    return jax.shard_map(shards, mesh=mesh, in_specs=in_specs, out_specs=out_specs, check_vma=False)
```

```python
import functools

import jax
import jax.numpy as jnp
from jax import lax
from jax.experimental import pallas as pl
from jax.experimental.pallas import tpu as pltpu
from jax.sharding import PartitionSpec as P

MESH = pl.DeviceIdType.MESH
F32, BF16 = jnp.float32, jnp.bfloat16
HI = lax.Precision.HIGHEST

HEADS, SLICES, DIM = 8, 64, 32
WIDTH = HEADS * DIM
COLS = HEADS * SLICES
NX, NY, NZ, NC = 4, 4, 16, 2
NXY = NX * NY
LOW = 4
NZH = NZ // LOW
ROWS1, ROWS2 = 9, 19
SMALL = 40
VMEM_BYTES = 60 * 1024 * 1024
BF_MAX = 3.3895314e38


def dot(a, b, ca=1, cb=0, precision=None):
    return lax.dot_general(
        a, b, (((ca,), (cb,)), ((), ())), preferred_element_type=F32, precision=precision
    )


def iota(shape, dim):
    return lax.broadcasted_iota(jnp.int32, shape, dim)


def split(values):
    high = values.astype(BF16)
    return high, (values - high.astype(F32)).astype(BF16)


def group_sum(high, low, ones):
    parts = []
    for g in range(0, COLS, 256):
        parts.append(dot(high[:, g : g + 256], ones) + dot(low[:, g : g + 256], ones))
    return jnp.concatenate(parts, axis=1)


def block_diagonal(tile_t):
    whole = jnp.concatenate([tile_t] * HEADS, axis=0)
    own = iota((WIDTH, COLS), 0) // DIM == iota((WIDTH, COLS), 1) // SLICES
    return jnp.where(own, whole, 0.0)


def diagonal_rows(full):
    left = iota((DIM, 128), 1) < SLICES
    parts = []
    for g in range(HEADS // 2):
        cols = slice(128 * g, 128 * g + 128)
        parts.append(
            jnp.where(
                left,
                full[2 * DIM * g : 2 * DIM * g + DIM, cols],
                full[2 * DIM * g + DIM : 2 * DIM * g + 2 * DIM, cols],
            )
        )
    return parts


def thirds(values):
    first = values.astype(BF16)
    rest = values - first.astype(F32)
    second = rest.astype(BF16)
    return first, second, (rest - second.astype(F32)).astype(BF16)


def left_terms(parts, axis=0):
    a, b, c = parts
    return jnp.concatenate([a, a, b, a, b, c], axis=axis)


def right_terms(parts, axis=0):
    a, b, c = parts
    return jnp.concatenate([a, b, a, c, b, a], axis=axis)


def weight_terms(weights):
    terms = [part.astype(F32) for part in thirds(weights)]
    return left_terms(terms, 1).astype(BF16)


def pair_dot(left, right, cb):
    a, b = split(left)
    c, d = split(right)
    return dot(jnp.concatenate([a, a, b], axis=1), jnp.concatenate([c, d, c], axis=cb), 1, cb)


def token_step(totals, masses, d_mixed, forward_terms, backward_terms):
    scale = DIM ** (-0.5)
    inv = 1.0 / (masses + 1e-05)
    tokens = totals * inv
    qkv = dot(forward_terms, right_terms(thirds(tokens)))
    q, k, v = qkv[:DIM], qkv[DIM : 2 * DIM], qkv[2 * DIM :]
    q_terms, k_terms = left_terms(thirds(q)), right_terms(thirds(k))
    m_terms, v_terms = left_terms(thirds(d_mixed)), right_terms(thirds(v))
    same = iota((128, 128), 0) // SLICES == iota((128, 128), 1) // SLICES
    mixed, dq, dk, dv = [], [], [], []
    for g in range(HEADS // 2):
        cols = slice(128 * g, 128 * g + 128)
        scores = dot(q_terms[:, cols], k_terms[:, cols], 0, 0) * scale
        d_att = dot(m_terms[:, cols], v_terms[:, cols], 0, 0)
        powers = jnp.where(same, jnp.exp(scores), 0.0)
        att = powers / jnp.sum(powers, axis=1, keepdims=True)
        d_scores = att * (d_att - jnp.sum(d_att * att, axis=1, keepdims=True)) * scale
        mixed.append(pair_dot(v[:, cols], att, 1))
        dq.append(pair_dot(k[:, cols], d_scores, 1))
        dk.append(pair_dot(q[:, cols], d_scores, 0))
        dv.append(pair_dot(d_mixed[:, cols], att, 0))
    mixed = jnp.concatenate(mixed, axis=1)
    backs = [jnp.concatenate(d, axis=1) for d in (dq, dk, dv)]
    d_tokens = dot(
        backward_terms, jnp.concatenate([right_terms(thirds(d)) for d in backs], axis=0)
    )
    d_masses = -jnp.sum(d_tokens * tokens, axis=0, keepdims=True) * inv
    return mixed, d_tokens * inv, d_masses, tokens, backs


def far_first(a):
    return (2 - a + 3 * (a // 2) - 2 * (a // 3)) % 4


def kernel(
    everyone,
    chunk,
    points_h,
    out_grad_h,
    gain_h,
    bias_h,
    w_mid_h,
    w_feat_h,
    w_slice_h,
    temper_h,
    wq_h,
    wk_h,
    wv_h,
    w_out_h,
    h_points,
    h_gain,
    h_bias,
    h_mid,
    h_feat,
    h_slice,
    h_temper,
    h_q,
    h_k,
    h_v,
    h_out,
    o_points,
    o_gain,
    o_bias,
    o_mid,
    o_feat,
    o_slice,
    o_temper,
    o_q,
    o_k,
    o_v,
    o_out,
    stores,
    points,
    out_grad,
    gain_ref,
    bias_ref,
    w_mid,
    w_feat,
    w_slice,
    temper,
    wq,
    wk,
    wv,
    w_out,
    loads,
    xhat_s,
    rstd_s,
    normed_s,
    mid_s,
    fd_s,
    low_s,
    logits_s,
    w_s,
    sw_s,
    sc_s,
    dmf_s,
    dn_s,
    p1,
    r10,
    a1,
    r11,
    r12,
    r13,
    pa,
    ra0,
    aa,
    ra1,
    ra2,
    ra3,
    ra4,
    pb,
    rb0,
    ab,
    rb1,
    rb2,
    rb3,
    pp,
    rp0,
    ap,
    rp1,
    sp,
    rp2,
    rp3,
    rp4,
    mb_s,
    sends,
    recvs,
):
    held = (
        (points_h, points),
        (w_mid_h, w_mid),
        (w_feat_h, w_feat),
        (gain_h, gain_ref),
        (bias_h, bias_ref),
        (w_slice_h, w_slice),
        (temper_h, temper),
        (out_grad_h, out_grad),
        (w_out_h, w_out),
        (wq_h, wq),
        (wk_h, wk),
        (wv_h, wv),
    )
    copies = [pltpu.make_async_copy(a, b, loads.at[n]) for n, (a, b) in enumerate(held)]
    for copy in copies:
        copy.start()

    p, c = lax.axis_index("pts"), lax.axis_index("rep")
    x, y, z = p // (NY * NZ), p // NZ % NY, p % NZ
    xy = x * NY + y
    zl, zh = z % LOW, z // LOW
    rows = points.shape[0]

    def plane_index(i):
        return (x + far_first(i // 4)) % NX * NY + (y + far_first(i % 4)) % NY

    def plane(i):
        return (plane_index(i) * NZ + z, c)

    def plane_cores(i):
        return (plane_index(i // 2) * NZ + z, (c + 1 + i % 2) % NC)

    def column_index(i):
        return (z + 8 + (i + 1) // 2 * (1 - 2 * (i % 2))) % NZ

    def column(i):
        return (xy * NZ + column_index(i), c)

    def low_index(i):
        return (zl + far_first(i)) % LOW

    def column_low(i):
        return (xy * NZ + zh * LOW + low_index(i), c)

    def column_high(i):
        return (xy * NZ + (z + LOW * far_first(i)) % NZ, c)

    sibling = (p, 1 - c)
    made = (
        (o_points, h_points),
        (o_gain, h_gain),
        (o_bias, h_bias),
        (o_mid, h_mid),
        (o_feat, h_feat),
        (o_slice, h_slice),
        (o_temper, h_temper),
        (o_q, h_q),
        (o_k, h_k),
        (o_v, h_v),
        (o_out, h_out),
    )
    writes = [pltpu.make_async_copy(a, b, stores.at[n]) for n, (a, b) in enumerate(made)]

    barrier = pltpu.get_barrier_semaphore()

    greetings = [(plane_cores, i) for i in range(2 * NXY - 1)]
    greetings += [(column, i) for i in range(NZ - 1)]
    n_greetings = len(greetings)

    def greet(count):
        for who, i in greetings[:count]:
            pl.semaphore_signal(barrier, inc=1, device_id=who(i), device_id_type=MESH)
        del greetings[:count]

    unsent, started = [], []

    def pack(ref, grad):
        for h in range(NC):
            for l in range(2):
                ref[h, 8 * l : 8 * l + 8, 0:16, :] = grad[
                    128 * h : 128 * h + 128, 128 * l : 128 * l + 128
                ].reshape(8, 16, 128)

    def unpack(ref, out):
        for l in range(2):
            out[:, 128 * l : 128 * l + 128] = ref[8 * l : 8 * l + 8, 0:16, :].reshape(128, 128)

    def send_all(stage, who, count, src, dst):
        def body(i, _):
            pltpu.make_async_remote_copy(
                src(i), dst, sends.at[stage], recvs.at[stage], device_id=who(i), device_id_type=MESH
            ).start()
            return 0

        lax.fori_loop(0, count, body, 0)

    def swap(stage, src, dst):
        send_all(stage, lambda i: sibling, 1, lambda i: src, dst)

    def wait(stage, ref):
        copy = pltpu.make_async_remote_copy(
            ref, ref, sends.at[stage], recvs.at[stage], device_id=sibling, device_id_type=MESH
        )
        copy.wait_recv()
        unsent.append(copy)

    def write(n):
        writes[n].start()
        started.append(writes[n])

    ones = (iota((256, 256), 0) // SLICES == iota((256, 256), 1) // SLICES).astype(F32).astype(BF16)

    with jax.named_scope("load"):
        for copy in copies[:7]:
            copy.wait()
    gain, bias = gain_ref[...], bias_ref[...]
    head_of = iota((1, COLS), 1) // SLICES
    temper_row = jnp.zeros((1, COLS), F32)
    for h in range(HEADS):
        temper_row = jnp.where(head_of == h, temper[:, h : h + 1], temper_row)
    inv_t = 1.0 / temper_row
    ws = w_slice[...].astype(F32)
    slice_blocks = block_diagonal(jnp.concatenate([ws] * HEADS, axis=1)).astype(BF16)

    with jax.named_scope("front"):
        for r in range(0, rows, chunk):
            here = pl.ds(r, chunk)
            greet(-(-n_greetings * chunk // rows))
            xs = points[here, :].astype(F32)
            center = xs - jnp.mean(xs, axis=1, keepdims=True)
            rstd = lax.rsqrt(jnp.mean(center * center, axis=1, keepdims=True) + 1e-05)
            xhat = center * rstd
            xhat_s[here, :] = xhat
            rstd_s[here, :] = jnp.broadcast_to(rstd, (chunk, 128))
            normed = (xhat * gain + bias).astype(BF16)
            normed_s[here, :] = normed
            mid = dot(normed, w_mid[...]).astype(BF16)
            mid_s[here, :] = mid
            fd_s[here, WIDTH:] = dot(normed, w_feat[...]).astype(BF16)
            logits = dot(mid, slice_blocks) * inv_t
            logits_s[here, :] = logits
            powers = jnp.exp(logits)
            high = jnp.minimum(powers, BF_MAX).astype(BF16)
            low = (powers - high.astype(F32)).astype(BF16)
            weights = powers / group_sum(high, low, ones)
            w_s[here, :] = weights
            sw_s[here, :] = weights.astype(BF16)
        for copy in copies[7:]:
            copy.wait()
        for r in range(0, rows, chunk):
            here = pl.ds(r, chunk)
            d_high, d_low = split(dot(out_grad[here, :], w_out[...], 1, 1))
            fd_s[here, :WIDTH] = d_high
            low_s[here, :] = d_low

    with jax.named_scope("shares1"):
        sw = sw_s[...]
        by_fd = dot(fd_s[...], sw, 0, 0)
        by_low = dot(low_s[...], sw, 0, 0)
        tot = diagonal_rows(by_fd[WIDTH:])
        dmx = diagonal_rows(by_fd[:WIDTH] + by_low)
        mass = dot(jnp.ones((8, rows), BF16), sw)[:1]
        quarter = iota((1, 128), 1) // DIM
        for i in range(4):
            for j in range(4):
                k = 4 * i + j
                p1[0, k, 0:8, :] = tot[j][8 * i : 8 * i + 8]
                p1[1, k, 0:8, :] = dmx[j][8 * i : 8 * i + 8]
                p1[0, k, 8:9, :] = jnp.where(quarter == i, mass[:, 128 * j : 128 * j + 128], 0.0)
                p1[1, k, 8:9, :] = jnp.zeros((1, 128), F32)

    with jax.named_scope("barrier"):
        pl.semaphore_wait(barrier, n_greetings)

    with jax.named_scope("sum1_core"):
        swap(0, p1.at[1 - c], r10)
        token_weights = (wq[...], wk[...], wv[...])
        forward_terms = jnp.concatenate([weight_terms(w.T) for w in token_weights], axis=0)
        backward_terms = jnp.concatenate([weight_terms(w) for w in token_weights], axis=1)
        projected = dot(out_grad[...], sw, 0, 0)
        for h in range(NC):
            half = projected[:, WIDTH * h : WIDTH * h + WIDTH]
            pp[h] = half.reshape(NXY, 16, WIDTH)
        wait(0, r10)
        a1[...] = p1[c] + r10[...]
    with jax.named_scope("sum1_plane"):
        send_all(1, plane, NXY - 1, lambda i: a1.at[plane_index(i)], r11.at[xy])
        swap(13, pp.at[1 - c], rp0)
        r11[xy] = a1[xy]
        wait(1, r11.at[pl.ds(0, NXY - 1)])
        r12[z] = jnp.sum(r11[...], axis=0)
    with jax.named_scope("sum1_column"):
        send_all(2, column, NZ - 1, lambda i: r12.at[z], r12.at[z])
        wait(13, rp0)
        ap[...] = pp[c] + rp0[...]
        send_all(14, plane, NXY - 1, lambda i: ap.at[plane_index(i)], rp1.at[xy])
        rp1[xy] = ap[xy]
        wait(2, r12.at[pl.ds(0, NZ - 1)])
        me1 = c * NXY + xy
        r13[me1] = jnp.sum(r12[...], axis=0)
    with jax.named_scope("sum1_back"):
        send_all(3, plane_cores, 2 * NXY - 1, lambda i: r13.at[me1], r13.at[me1])
        wait(14, rp1.at[pl.ds(0, NXY - 1)])
        piece = jnp.sum(rp1[...], axis=0)
        for k in range(NZ):
            sp[k] = piece[k : k + 1]
        send_all(15, column, NZ - 1, lambda i: sp.at[column_index(i)], rp2.at[z])
        rp2[z] = sp[z]
        wait(3, r13.at[pl.ds(0, 2 * NXY - 1)])

    def whole(half):
        return jnp.concatenate(
            [
                jnp.concatenate([r13[NXY * half + 4 * i + j, 0:8, :] for i in range(4)], axis=0)
                for j in range(4)
            ],
            axis=1,
        )

    with jax.named_scope("tokens"):
        masses = jnp.concatenate(
            [sum(r13[4 * i + j, 8:9, :] for i in range(4)) for j in range(4)], axis=1
        )
        mixed, d_totals, d_masses, tokens, backs = token_step(
            whole(0), masses, whole(1), forward_terms, backward_terms
        )
        mixed_blocks = block_diagonal(mixed.astype(BF16).astype(F32)).astype(BF16)
        totals_blocks = block_diagonal(d_totals.astype(BF16).astype(F32)).astype(BF16)
        both = jnp.concatenate([mixed_blocks, totals_blocks], axis=0)
        for h in range(NC):
            mb_s[h] = mixed_blocks[128 * h : 128 * h + 128, WIDTH * h : WIDTH * h + WIDTH]

    with jax.named_scope("feat"):
        for r in range(0, rows, chunk):
            here = pl.ds(r, chunk)
            dmf_s[here, WIDTH:] = dot(sw_s[here, :], totals_blocks, 1, 1).astype(BF16)
        pack(pa, dot(normed_s[...], dmf_s[:, WIDTH:], 0, 0))
        swap(4, pa.at[1 - c], ra0)

    with jax.named_scope("out"):
        wait(15, rp2.at[pl.ds(0, NZ - 1)])
        row_high, row_low = split(jnp.broadcast_to(jnp.sum(rp2[...], axis=0), (16, WIDTH)))
        own = dot(row_high, mb_s[c], 1, 1) + dot(row_low, mb_s[c], 1, 1)
        rp3[z] = own[:1] / everyone
        send_all(16, column, NZ - 1, lambda i: rp3.at[z], rp3.at[z])

    w_both = jnp.concatenate([w_mid[...], w_feat[...]], axis=1)

    def fold(values):
        return jnp.sum(values.reshape(values.shape[0] // 8, 8, values.shape[1]), axis=0)

    sums = [jnp.zeros((8, COLS), F32), jnp.zeros((8, WIDTH), F32), jnp.zeros((8, WIDTH), F32)]

    def back(r):
        here = pl.ds(r, chunk)
        weights = w_s[here, :]
        d_weights = dot(fd_s[here, :], both) + d_masses
        high, low = split(d_weights * weights)
        d_logits = weights * (d_weights - group_sum(high, low, ones))
        scaled = (d_logits * inv_t).astype(BF16)
        sc_s[here, :] = scaled
        sums[0] += fold(d_logits * logits_s[here, :])
        dmf_s[here, :WIDTH] = dot(scaled, slice_blocks, 1, 1).astype(BF16)
        d_normed = dot(dmf_s[here, :], w_both, 1, 1)
        dn_s[here, :] = d_normed
        sums[1] += fold(d_normed * xhat_s[here, :])
        sums[2] += fold(d_normed)

    with jax.named_scope("back_first"):
        for r in range(0, rows // 2, chunk):
            back(r)
    with jax.named_scope("suma_core"):
        wait(4, ra0)
        aa[...] = pa[c] + ra0[...]
        send_all(5, plane, NXY - 1, lambda i: aa.at[plane_index(i)], ra1.at[xy])
        ra1[xy] = aa[xy]
    with jax.named_scope("back_second"):
        for r in range(rows // 2, rows, chunk):
            back(r)
    with jax.named_scope("sharesb"):
        grad_mid = dot(normed_s[...], dmf_s[:, :WIDTH], 0, 0)
        slice_sum = sum(diagonal_rows(dot(mid_s[...], sc_s[...], 0, 0)))
        temper_sum, gain_sum, bias_sum = (jnp.sum(v, axis=0, keepdims=True) for v in sums)
        small = [gain_sum[:, 128 * l : 128 * l + 128] for l in range(2)]
        small += [bias_sum[:, 128 * l : 128 * l + 128] for l in range(2)]
        small += [temper_sum[:, 128 * l : 128 * l + 128] for l in range(4)]
        small += [slice_sum[d : d + 1] for d in range(DIM)]
        small += [jnp.zeros((1, 128), F32)] * (3 * NXY - len(small))
        small = jnp.concatenate(small, axis=0)
        pack(pb, grad_mid)
        for h in range(NC):
            for k in range(NXY):
                pb[h, k, 16:19, :] = small[3 * k : 3 * k + 3]

    with jax.named_scope("sumb_core"):
        swap(9, pb.at[1 - c], rb0)
    with jax.named_scope("sumb_plane"):
        wait(9, rb0)
        ab[...] = pb[c] + rb0[...]
        send_all(10, plane, NXY - 1, lambda i: ab.at[plane_index(i)], rb1.at[xy])
        rb1[xy] = ab[xy]
    with jax.named_scope("suma_plane"):
        wait(5, ra1.at[pl.ds(0, NXY - 1)])
        ra2[zl] = jnp.sum(ra1[...], axis=0)
        send_all(6, column_low, LOW - 1, lambda i: ra2.at[zl], ra2.at[zl])

    with jax.named_scope("points"):
        for r in range(0, rows, chunk):
            here = pl.ds(r, chunk)
            xhat = xhat_s[here, :]
            d_xhat = dn_s[here, :] * gain
            inner = d_xhat - jnp.mean(d_xhat, axis=1, keepdims=True)
            inner = inner - xhat * jnp.mean(d_xhat * xhat, axis=1, keepdims=True)
            o_points[here, :] = (inner * rstd_s[here, 0:1]).astype(BF16)
        write(0)

    with jax.named_scope("suma_low"):
        wait(6, ra2.at[pl.ds(0, LOW - 1)])
        ra3[zh] = jnp.sum(ra2[...], axis=0)
        send_all(7, column_high, NZH - 1, lambda i: ra3.at[zh], ra3.at[zh])
    with jax.named_scope("sumb_column"):
        wait(10, rb1.at[pl.ds(0, NXY - 1)])
        rb2[z] = jnp.sum(rb1[...], axis=0)
        send_all(11, column, NZ - 1, lambda i: rb2.at[z], rb2.at[z])
    with jax.named_scope("out_column"):
        wait(16, rp3.at[pl.ds(0, NZ - 1)])
        rp4[xy] = jnp.concatenate([rp3[k] for k in range(NZ)], axis=0)
        send_all(17, plane, NXY - 1, lambda i: rp4.at[xy], rp4.at[xy])
    with jax.named_scope("token_grads"):
        for n, out, back in zip((7, 8, 9), (o_q, o_k, o_v), backs):
            out[...] = dot(tokens, back, 1, 1, HI) / everyone
            write(n)
    with jax.named_scope("suma_high"):
        wait(7, ra3.at[pl.ds(0, NZH - 1)])
        ra4[xy] = jnp.sum(ra3[...], axis=0) / everyone
        send_all(8, plane, NXY - 1, lambda i: ra4.at[xy], ra4.at[xy])
    with jax.named_scope("out_last"):
        wait(17, rp4.at[pl.ds(0, NXY - 1)])
        o_out[...] = rp4[...].reshape(WIDTH, 128).T
        write(10)
    with jax.named_scope("sumb_back"):
        wait(11, rb2.at[pl.ds(0, NZ - 1)])
        rb3[xy] = jnp.sum(rb2[...], axis=0) / everyone
        send_all(12, plane, NXY - 1, lambda i: rb3.at[xy], rb3.at[xy])
    with jax.named_scope("suma_last"):
        wait(8, ra4.at[pl.ds(0, NXY - 1)])
        unpack(ra4, o_feat)
        write(4)
    with jax.named_scope("sumb_last"):
        wait(12, rb3.at[pl.ds(0, NXY - 1)])
        unpack(rb3, o_mid)
        small = [rb3[k // 3, 16 + k % 3 : 17 + k % 3, :] for k in range(SMALL)]
        for l in range(2):
            o_gain[:, 128 * l : 128 * l + 128] = small[l]
            o_bias[:, 128 * l : 128 * l + 128] = small[2 + l]
        folded = jnp.concatenate(small[8:], axis=0)
        o_slice[...] = (folded + pltpu.roll(folded, SLICES, 1))[:, :SLICES]
        lane, place = iota((1, 128), 1), iota((1, HEADS), 1)
        d_temper = jnp.zeros((1, HEADS), F32)
        for g in range(4):
            for s in range(2):
                part = jnp.where(lane // SLICES == s, small[4 + g], 0.0)
                part = jnp.sum(part, axis=1, keepdims=True)
                d_temper = jnp.where(place == 2 * g + s, part, d_temper)
        o_temper[...] = -d_temper / temper[...]
        for n in (1, 2, 3, 5, 6):
            write(n)

    with jax.named_scope("done"):
        for copy in unsent:
            copy.wait_send()
        for copy in started:
            copy.wait()


def hand_on(count, *refs):
    ins, outs, held, (loads, stores) = (
        refs[:count],
        refs[count : 2 * count],
        refs[2 * count : 3 * count],
        refs[3 * count :],
    )
    one = [pltpu.make_async_copy(ins[n], held[n], loads.at[n]) for n in range(count)]
    two = [pltpu.make_async_copy(held[n], outs[n], stores.at[n]) for n in range(count)]
    for copy in one:
        copy.start()
    for first, second in zip(one, two):
        first.wait()
        second.start()
    for copy in two:
        copy.wait()


def shards(
    points, out_grad, ln_gain, ln_bias, w_mid, w_feat, w_slice, temper, wq, wk, wv, w_out
):
    rows = points.shape[0]
    everyone = rows * NXY * NZ * NC
    hbm = pl.BlockSpec(memory_space=pltpu.HBM)
    f = lambda *s: jax.ShapeDtypeStruct(s, F32)
    args = (
        points,
        out_grad,
        ln_gain.reshape(1, -1),
        ln_bias.reshape(1, -1),
        w_mid,
        w_feat,
        w_slice,
        temper.reshape(1, -1),
        wq,
        wk,
        wv,
        w_out,
    )
    out_shape = (
        jax.ShapeDtypeStruct((rows, WIDTH), BF16),
        f(1, WIDTH),
        f(1, WIDTH),
        f(128, WIDTH),
        f(128, WIDTH),
        f(DIM, SLICES),
        f(1, HEADS),
        f(DIM, DIM),
        f(DIM, DIM),
        f(DIM, DIM),
        f(128, WIDTH),
    )
    outs = pl.pallas_call(
        functools.partial(kernel, float(everyone), 128),
        out_shape=out_shape,
        in_specs=[hbm] * 12,
        out_specs=(hbm,) * 11,
        scratch_shapes=[pltpu.VMEM(a.shape, a.dtype) for a in out_shape]
        + [pltpu.SemaphoreType.DMA((11,))]
        + [pltpu.VMEM(a.shape, a.dtype) for a in args]
        + [pltpu.SemaphoreType.DMA((12,))]
        + [
            pltpu.VMEM((rows, WIDTH), F32),
            pltpu.VMEM((rows, 128), F32),
            pltpu.VMEM((rows, WIDTH), BF16),
            pltpu.VMEM((rows, WIDTH), BF16),
            pltpu.VMEM((rows, 2 * WIDTH), BF16),
            pltpu.VMEM((rows, WIDTH), BF16),
            pltpu.VMEM((rows, COLS), F32),
            pltpu.VMEM((rows, COLS), F32),
            pltpu.VMEM((rows, COLS), BF16),
            pltpu.VMEM((rows, COLS), BF16),
            pltpu.VMEM((rows, 2 * WIDTH), BF16),
            pltpu.VMEM((rows, WIDTH), F32),
        ]
        + [
            pltpu.VMEM(lead + (ROWS1, 128), F32)
            for lead in ((NC, NXY), (NXY,), (NXY,), (NXY,), (NZ,), (NC * NXY,))
        ]
        + [
            pltpu.VMEM(lead + (16, 128), F32)
            for lead in ((NC, NXY), (NXY,), (NXY,), (NXY,), (LOW,), (NZH,), (NXY,))
        ]
        + [
            pltpu.VMEM(lead + (ROWS2, 128), F32)
            for lead in ((NC, NXY), (NXY,), (NXY,), (NXY,), (NZ,), (NXY,))
        ]
        + [
            pltpu.VMEM((NC, NXY, 16, WIDTH), F32),
            pltpu.VMEM((NXY, 16, WIDTH), F32),
            pltpu.VMEM((NXY, 16, WIDTH), F32),
            pltpu.VMEM((NXY, 16, WIDTH), F32),
            pltpu.VMEM((NZ, 1, WIDTH), F32),
            pltpu.VMEM((NZ, 1, WIDTH), F32),
            pltpu.VMEM((NZ, 1, 128), F32),
            pltpu.VMEM((NXY, 16, 128), F32),
            pltpu.VMEM((NC, 128, WIDTH), BF16),
        ]
        + [pltpu.SemaphoreType.DMA((18,)), pltpu.SemaphoreType.DMA((18,))],
        compiler_params=pltpu.CompilerParams(
            collective_id=0, has_side_effects=True, vmem_limit_bytes=VMEM_BYTES
        ),
        name="backward",
    )(*args)
    outs = pl.pallas_call(
        functools.partial(hand_on, len(outs)),
        out_shape=out_shape,
        in_specs=[hbm] * 11,
        out_specs=(hbm,) * 11,
        scratch_shapes=[pltpu.VMEM(a.shape, a.dtype) for a in out_shape]
        + [pltpu.SemaphoreType.DMA((11,))] * 2,
        compiler_params=pltpu.CompilerParams(vmem_limit_bytes=VMEM_BYTES),
        name="hand_on",
    )(*outs)
    outs = list(outs)
    for n in (1, 2, 6):
        outs[n] = outs[n].reshape(-1)
    return tuple(outs)


def solution(mesh):
    by_point, by_rep = P(("pts", "rep"), None), P("rep", None)
    in_specs = (by_point, by_point) + (P(),) * 10
    out_specs = (by_point, P(), P(), by_rep, by_rep, P(), P(), P(), P(), P(), by_rep)
    return jax.shard_map(shards, mesh=mesh, in_specs=in_specs, out_specs=out_specs, check_vma=False)
```

```python
import functools

import jax
import jax.numpy as jnp
from jax import lax
from jax.experimental import pallas as pl
from jax.experimental.pallas import tpu as pltpu
from jax.sharding import PartitionSpec as P

MESH = pl.DeviceIdType.MESH
F32, BF16 = jnp.float32, jnp.bfloat16
HI = lax.Precision.HIGHEST

HEADS, SLICES, DIM = 8, 64, 32
WIDTH = HEADS * DIM
COLS = HEADS * SLICES
NX, NY, NZ, NC = 4, 4, 16, 2
NXY = NX * NY
LOW = 4
NZH = NZ // LOW
ROWS1, ROWS2, ROWS3 = 9, 16, 3
SMALL = 40
VMEM_BYTES = 48 * 1024 * 1024
BF_MAX = 3.3895314e38


def dot(a, b, ca=1, cb=0, precision=None):
    return lax.dot_general(
        a, b, (((ca,), (cb,)), ((), ())), preferred_element_type=F32, precision=precision
    )


def iota(shape, dim):
    return lax.broadcasted_iota(jnp.int32, shape, dim)


def split(values):
    high = values.astype(BF16)
    return high, (values - high.astype(F32)).astype(BF16)


def group_sum(high, low, ones):
    parts = []
    for g in range(0, COLS, 256):
        parts.append(dot(high[:, g : g + 256], ones) + dot(low[:, g : g + 256], ones))
    return jnp.concatenate(parts, axis=1)


def block_diagonal(tile_t):
    whole = jnp.concatenate([tile_t] * HEADS, axis=0)
    own = iota((WIDTH, COLS), 0) // DIM == iota((WIDTH, COLS), 1) // SLICES
    return jnp.where(own, whole, 0.0)


def diagonal_rows(full):
    left = iota((DIM, 128), 1) < SLICES
    parts = []
    for g in range(HEADS // 2):
        cols = slice(128 * g, 128 * g + 128)
        parts.append(
            jnp.where(
                left,
                full[2 * DIM * g : 2 * DIM * g + DIM, cols],
                full[2 * DIM * g + DIM : 2 * DIM * g + 2 * DIM, cols],
            )
        )
    return parts


def thirds(values):
    first = values.astype(BF16)
    rest = values - first.astype(F32)
    second = rest.astype(BF16)
    return first, second, (rest - second.astype(F32)).astype(BF16)


def left_terms(parts, axis=0):
    a, b, c = parts
    return jnp.concatenate([a, a, b, a, b, c], axis=axis)


def right_terms(parts, axis=0):
    a, b, c = parts
    return jnp.concatenate([a, b, a, c, b, a], axis=axis)


def weight_terms(weights):
    terms = [part.astype(F32) for part in thirds(weights)]
    return left_terms(terms, 1).astype(BF16)


def pair_dot(left, right, cb):
    a, b = split(left)
    c, d = split(right)
    return dot(jnp.concatenate([a, a, b], axis=1), jnp.concatenate([c, d, c], axis=cb), 1, cb)


def token_step(totals, masses, d_mixed, forward_terms, backward_terms):
    scale = DIM ** (-0.5)
    inv = 1.0 / (masses + 1e-05)
    tokens = totals * inv
    qkv = dot(forward_terms, right_terms(thirds(tokens)))
    q, k, v = qkv[:DIM], qkv[DIM : 2 * DIM], qkv[2 * DIM :]
    q_terms, k_terms = left_terms(thirds(q)), right_terms(thirds(k))
    m_terms, v_terms = left_terms(thirds(d_mixed)), right_terms(thirds(v))
    same = iota((128, 128), 0) // SLICES == iota((128, 128), 1) // SLICES
    mixed, dq, dk, dv = [], [], [], []
    for g in range(HEADS // 2):
        cols = slice(128 * g, 128 * g + 128)
        scores = dot(q_terms[:, cols], k_terms[:, cols], 0, 0) * scale
        d_att = dot(m_terms[:, cols], v_terms[:, cols], 0, 0)
        powers = jnp.where(same, jnp.exp(scores), 0.0)
        att = powers / jnp.sum(powers, axis=1, keepdims=True)
        d_scores = att * (d_att - jnp.sum(d_att * att, axis=1, keepdims=True)) * scale
        mixed.append(pair_dot(v[:, cols], att, 1))
        dq.append(pair_dot(k[:, cols], d_scores, 1))
        dk.append(pair_dot(q[:, cols], d_scores, 0))
        dv.append(pair_dot(d_mixed[:, cols], att, 0))
    mixed = jnp.concatenate(mixed, axis=1)
    backs = [jnp.concatenate(d, axis=1) for d in (dq, dk, dv)]
    d_tokens = dot(
        backward_terms, jnp.concatenate([right_terms(thirds(d)) for d in backs], axis=0)
    )
    d_masses = -jnp.sum(d_tokens * tokens, axis=0, keepdims=True) * inv
    return mixed, d_tokens * inv, d_masses, tokens, backs


def far_first(a):
    return (2 - a + 3 * (a // 2) - 2 * (a // 3)) % 4


def kernel(
    everyone,
    chunk,
    points_h,
    out_grad_h,
    gain_h,
    bias_h,
    w_mid_h,
    w_feat_h,
    w_slice_h,
    temper_h,
    wq_h,
    wk_h,
    wv_h,
    w_out_h,
    o_points,
    o_gain,
    o_bias,
    o_mid,
    o_feat,
    o_slice,
    o_temper,
    o_q,
    o_k,
    o_v,
    o_out,
    points,
    out_grad,
    gain_ref,
    bias_ref,
    w_mid,
    w_feat,
    w_slice,
    temper,
    wq,
    wk,
    wv,
    w_out,
    loads,
    xhat_s,
    rstd_s,
    normed_s,
    mid_s,
    fd_s,
    low_s,
    logits_s,
    w_s,
    sw_s,
    sc_s,
    dmf_s,
    dn_s,
    p1,
    r11,
    r12,
    r13,
    pa,
    ra0,
    aa,
    ra1,
    ra2,
    ra3,
    ra4,
    pb,
    rb0,
    ab,
    rb1,
    rb2,
    rb3,
    pp,
    rp0,
    ap,
    rp1,
    sp,
    rp2,
    rp3,
    rp4,
    mb_s,
    ps,
    rs0,
    as_,
    rs1,
    rs2,
    rs3,
    sends,
    recvs,
):
    held = (
        (points_h, points),
        (w_mid_h, w_mid),
        (w_feat_h, w_feat),
        (gain_h, gain_ref),
        (bias_h, bias_ref),
        (w_slice_h, w_slice),
        (temper_h, temper),
        (out_grad_h, out_grad),
        (w_out_h, w_out),
        (wq_h, wq),
        (wk_h, wk),
        (wv_h, wv),
    )
    copies = [pltpu.make_async_copy(a, b, loads.at[n]) for n, (a, b) in enumerate(held)]
    for copy in copies:
        copy.start()

    p, c = lax.axis_index("pts"), lax.axis_index("rep")
    x, y, z = p // (NY * NZ), p // NZ % NY, p % NZ
    xy = x * NY + y
    zl, zh = z % LOW, z // LOW
    rows = points.shape[0]

    def plane_index(i):
        return (x + far_first(i // 4)) % NX * NY + (y + far_first(i % 4)) % NY

    def plane(i):
        return (plane_index(i) * NZ + z, c)

    def plane_cores(i):
        return (plane_index(i // 2) * NZ + z, (c + 1 + i % 2) % NC)

    def column_index(i):
        return (z + 8 + (i + 1) // 2 * (1 - 2 * (i % 2))) % NZ

    def column(i):
        return (xy * NZ + column_index(i), c)

    def low_index(i):
        return (zl + far_first(i)) % LOW

    def column_low(i):
        return (xy * NZ + zh * LOW + low_index(i), c)

    def column_high(i):
        return (xy * NZ + (z + LOW * far_first(i)) % NZ, c)

    sibling = (p, 1 - c)
    barrier = pltpu.get_barrier_semaphore()

    greetings = [(plane_cores, i) for i in range(2 * NXY - 1)]
    greetings += [(column, i) for i in range(NZ - 1)]
    n_greetings = len(greetings)

    def greet(count):
        for who, i in greetings[:count]:
            pl.semaphore_signal(barrier, inc=1, device_id=who(i), device_id_type=MESH)
        del greetings[:count]

    with jax.named_scope("greet"):
        greet(n_greetings)

    unsent = []

    def pack(ref, grad):
        for h in range(NC):
            for l in range(2):
                ref[h, 8 * l : 8 * l + 8, 0:16, :] = grad[
                    128 * h : 128 * h + 128, 128 * l : 128 * l + 128
                ].reshape(8, 16, 128)

    def unpack(ref, out):
        for l in range(2):
            out[:, 128 * l : 128 * l + 128] = ref[8 * l : 8 * l + 8, 0:16, :].reshape(128, 128)

    def send_all(stage, who, count, src, dst):
        def body(i, _):
            pltpu.make_async_remote_copy(
                src(i), dst, sends.at[stage], recvs.at[stage], device_id=who(i), device_id_type=MESH
            ).start()
            return 0

        lax.fori_loop(0, count, body, 0)

    def swap(stage, src, dst):
        send_all(stage, lambda i: sibling, 1, lambda i: src, dst)

    def wait(stage, ref):
        copy = pltpu.make_async_remote_copy(
            ref, ref, sends.at[stage], recvs.at[stage], device_id=sibling, device_id_type=MESH
        )
        copy.wait_recv()
        unsent.append(copy)

    ones = (iota((256, 256), 0) // SLICES == iota((256, 256), 1) // SLICES).astype(F32).astype(BF16)

    with jax.named_scope("load"):
        for copy in copies[:7]:
            copy.wait()
    gain, bias = gain_ref[...], bias_ref[...]
    head_of = iota((1, COLS), 1) // SLICES
    temper_row = jnp.zeros((1, COLS), F32)
    for h in range(HEADS):
        temper_row = jnp.where(head_of == h, temper[:, h : h + 1], temper_row)
    inv_t = 1.0 / temper_row
    ws = w_slice[...].astype(F32)
    slice_blocks = block_diagonal(jnp.concatenate([ws] * HEADS, axis=1)).astype(BF16)

    with jax.named_scope("front"):
        for r in range(0, rows, chunk):
            here = pl.ds(r, chunk)
            xs = points[here, :].astype(F32)
            center = xs - jnp.mean(xs, axis=1, keepdims=True)
            rstd = lax.rsqrt(jnp.mean(center * center, axis=1, keepdims=True) + 1e-05)
            xhat = center * rstd
            xhat_s[here, :] = xhat
            rstd_s[here, :] = jnp.broadcast_to(rstd, (chunk, 128))
            normed = (xhat * gain + bias).astype(BF16)
            normed_s[here, :] = normed
            mid = dot(normed, w_mid[...]).astype(BF16)
            mid_s[here, :] = mid
            fd_s[here, WIDTH:] = dot(normed, w_feat[...]).astype(BF16)
            logits = dot(mid, slice_blocks) * inv_t
            logits_s[here, :] = logits
            powers = jnp.exp(logits)
            high = jnp.minimum(powers, BF_MAX).astype(BF16)
            low = (powers - high.astype(F32)).astype(BF16)
            weights = powers / group_sum(high, low, ones)
            w_s[here, :] = weights
            sw_s[here, :] = weights.astype(BF16)
        for copy in copies[7:]:
            copy.wait()
        for r in range(0, rows, chunk):
            here = pl.ds(r, chunk)
            d_high, d_low = split(dot(out_grad[here, :], w_out[...], 1, 1))
            fd_s[here, :WIDTH] = d_high
            low_s[here, :] = d_low

    with jax.named_scope("shares1"):
        sw = sw_s[...]
        by_fd = dot(fd_s[...], sw, 0, 0)
        by_low = dot(low_s[...], sw, 0, 0)
        tot = diagonal_rows(by_fd[WIDTH:])
        dmx = diagonal_rows(by_fd[:WIDTH] + by_low)
        mass = dot(jnp.ones((8, rows), BF16), sw)[:1]
        quarter = iota((1, 128), 1) // DIM
        for i in range(4):
            for j in range(4):
                k = 4 * i + j
                p1[0, k, 0:8, :] = tot[j][8 * i : 8 * i + 8]
                p1[1, k, 0:8, :] = dmx[j][8 * i : 8 * i + 8]
                p1[0, k, 8:9, :] = jnp.where(quarter == i, mass[:, 128 * j : 128 * j + 128], 0.0)
                p1[1, k, 8:9, :] = jnp.zeros((1, 128), F32)

    with jax.named_scope("barrier"):
        pl.semaphore_wait(barrier, n_greetings)

    me1 = c * NXY + xy
    with jax.named_scope("sum1_plane"):
        send_all(
            1,
            plane_cores,
            2 * NXY - 1,
            lambda i: p1.at[(c + 1 + i % 2) % NC, plane_index(i // 2)],
            r11.at[me1],
        )
        r11[me1] = p1[c, xy]
        projected = dot(out_grad[...], sw, 0, 0)
        for h in range(NC):
            half = projected[:, WIDTH * h : WIDTH * h + WIDTH]
            pp[h] = half.reshape(NXY, 16, WIDTH)
        swap(13, pp.at[1 - c], rp0)
        token_weights = (wq[...], wk[...], wv[...])
        forward_terms = jnp.concatenate([weight_terms(w.T) for w in token_weights], axis=0)
        backward_terms = jnp.concatenate([weight_terms(w) for w in token_weights], axis=1)
        wait(1, r11.at[pl.ds(0, 2 * NXY - 1)])
        r12[z] = jnp.sum(r11[...], axis=0)
    with jax.named_scope("sum1_column"):
        send_all(2, column, NZ - 1, lambda i: r12.at[z], r12.at[z])
        wait(13, rp0)
        ap[...] = pp[c] + rp0[...]
        send_all(14, plane, NXY - 1, lambda i: ap.at[plane_index(i)], rp1.at[xy])
        rp1[xy] = ap[xy]
        wait(2, r12.at[pl.ds(0, NZ - 1)])
        r13[me1] = jnp.sum(r12[...], axis=0)
    with jax.named_scope("sum1_back"):
        send_all(3, plane_cores, 2 * NXY - 1, lambda i: r13.at[me1], r13.at[me1])
        wait(14, rp1.at[pl.ds(0, NXY - 1)])
        piece = jnp.sum(rp1[...], axis=0)
        for k in range(NZ):
            sp[k] = piece[k : k + 1]
        send_all(15, column, NZ - 1, lambda i: sp.at[column_index(i)], rp2.at[z])
        rp2[z] = sp[z]
        wait(3, r13.at[pl.ds(0, 2 * NXY - 1)])

    def whole(half):
        return jnp.concatenate(
            [
                jnp.concatenate([r13[NXY * half + 4 * i + j, 0:8, :] for i in range(4)], axis=0)
                for j in range(4)
            ],
            axis=1,
        )

    with jax.named_scope("tokens"):
        masses = jnp.concatenate(
            [sum(r13[4 * i + j, 8:9, :] for i in range(4)) for j in range(4)], axis=1
        )
        mixed, d_totals, d_masses, tokens, backs = token_step(
            whole(0), masses, whole(1), forward_terms, backward_terms
        )
        mixed_blocks = block_diagonal(mixed.astype(BF16).astype(F32)).astype(BF16)
        totals_blocks = block_diagonal(d_totals.astype(BF16).astype(F32)).astype(BF16)
        both = jnp.concatenate([mixed_blocks, totals_blocks], axis=0)
        for h in range(NC):
            mb_s[h] = mixed_blocks[128 * h : 128 * h + 128, WIDTH * h : WIDTH * h + WIDTH]

    with jax.named_scope("feat"):
        for r in range(0, rows, chunk):
            here = pl.ds(r, chunk)
            dmf_s[here, WIDTH:] = dot(sw_s[here, :], totals_blocks, 1, 1).astype(BF16)
        pack(pa, dot(normed_s[...], dmf_s[:, WIDTH:], 0, 0))
        swap(4, pa.at[1 - c], ra0)

    with jax.named_scope("out"):
        wait(15, rp2.at[pl.ds(0, NZ - 1)])
        row_high, row_low = split(jnp.broadcast_to(jnp.sum(rp2[...], axis=0), (16, WIDTH)))
        own = dot(row_high, mb_s[c], 1, 1) + dot(row_low, mb_s[c], 1, 1)
        rp3[z] = own[:1] / everyone
        send_all(16, column, NZ - 1, lambda i: rp3.at[z], rp3.at[z])

    w_both = jnp.concatenate([w_mid[...], w_feat[...]], axis=1)

    def fold(values):
        return jnp.sum(values.reshape(values.shape[0] // 8, 8, values.shape[1]), axis=0)

    sums = [jnp.zeros((8, COLS), F32), jnp.zeros((8, WIDTH), F32), jnp.zeros((8, WIDTH), F32)]

    def back(r):
        here = pl.ds(r, chunk)
        weights = w_s[here, :]
        d_weights = dot(fd_s[here, :], both) + d_masses
        high, low = split(d_weights * weights)
        d_logits = weights * (d_weights - group_sum(high, low, ones))
        scaled = (d_logits * inv_t).astype(BF16)
        sc_s[here, :] = scaled
        sums[0] += fold(d_logits * logits_s[here, :])
        dmf_s[here, :WIDTH] = dot(scaled, slice_blocks, 1, 1).astype(BF16)

    def norm(r):
        here = pl.ds(r, chunk)
        d_normed = dot(dmf_s[here, :], w_both, 1, 1)
        dn_s[here, :] = d_normed
        sums[1] += fold(d_normed * xhat_s[here, :])
        sums[2] += fold(d_normed)

    with jax.named_scope("back_first"):
        for r in range(0, rows // 2, chunk):
            back(r)
    with jax.named_scope("suma_core"):
        wait(4, ra0)
        aa[...] = pa[c] + ra0[...]
        send_all(5, plane, NXY - 1, lambda i: aa.at[plane_index(i)], ra1.at[xy])
        ra1[xy] = aa[xy]
    with jax.named_scope("back_second"):
        for r in range(rows // 2, rows, chunk):
            back(r)
    with jax.named_scope("sumb_core"):
        pack(pb, dot(normed_s[...], dmf_s[:, :WIDTH], 0, 0))
        swap(9, pb.at[1 - c], rb0)
    with jax.named_scope("shares_small"):
        for r in range(0, rows, chunk):
            norm(r)
        slice_sum = sum(diagonal_rows(dot(mid_s[...], sc_s[...], 0, 0)))
        temper_sum, gain_sum, bias_sum = (jnp.sum(v, axis=0, keepdims=True) for v in sums)
        small = [gain_sum[:, 128 * l : 128 * l + 128] for l in range(2)]
        small += [bias_sum[:, 128 * l : 128 * l + 128] for l in range(2)]
        small += [temper_sum[:, 128 * l : 128 * l + 128] for l in range(4)]
        small += [slice_sum, jnp.zeros((ROWS3 * NXY - SMALL, 128), F32)]
        small = jnp.concatenate(small, axis=0)
        for k in range(NXY):
            ps[k] = small[ROWS3 * k : ROWS3 * k + ROWS3]
        swap(0, ps, rs0)

    with jax.named_scope("sumb_plane"):
        wait(9, rb0)
        ab[...] = pb[c] + rb0[...]
        send_all(10, plane, NXY - 1, lambda i: ab.at[plane_index(i)], rb1.at[xy])
        rb1[xy] = ab[xy]
    with jax.named_scope("suma_plane"):
        wait(5, ra1.at[pl.ds(0, NXY - 1)])
        ra2[zl] = jnp.sum(ra1[...], axis=0)
        send_all(6, column_low, LOW - 1, lambda i: ra2.at[zl], ra2.at[zl])

    with jax.named_scope("small_plane"):
        wait(0, rs0)
        as_[...] = ps[...] + rs0[...]
        send_all(18, plane, NXY - 1, lambda i: as_.at[plane_index(i)], rs1.at[xy])
        rs1[xy] = as_[xy]
    with jax.named_scope("points"):
        for r in range(0, rows, chunk):
            here = pl.ds(r, chunk)
            xhat = xhat_s[here, :]
            d_xhat = dn_s[here, :] * gain
            inner = d_xhat - jnp.mean(d_xhat, axis=1, keepdims=True)
            inner = inner - xhat * jnp.mean(d_xhat * xhat, axis=1, keepdims=True)
            o_points[here, :] = (inner * rstd_s[here, 0:1]).astype(BF16)

    with jax.named_scope("suma_low"):
        wait(6, ra2.at[pl.ds(0, LOW - 1)])
        ra3[zh] = jnp.sum(ra2[...], axis=0)
        send_all(7, column_high, NZH - 1, lambda i: ra3.at[zh], ra3.at[zh])
    with jax.named_scope("sumb_column"):
        wait(10, rb1.at[pl.ds(0, NXY - 1)])
        rb2[z] = jnp.sum(rb1[...], axis=0)
        send_all(11, column, NZ - 1, lambda i: rb2.at[z], rb2.at[z])
    with jax.named_scope("out_column"):
        wait(16, rp3.at[pl.ds(0, NZ - 1)])
        rp4[xy] = jnp.concatenate([rp3[k] for k in range(NZ)], axis=0)
        send_all(17, plane, NXY - 1, lambda i: rp4.at[xy], rp4.at[xy])
    with jax.named_scope("small_column"):
        wait(18, rs1.at[pl.ds(0, NXY - 1)])
        rs2[z] = jnp.sum(rs1[...], axis=0)
        send_all(19, column, NZ - 1, lambda i: rs2.at[z], rs2.at[z])
    with jax.named_scope("token_grads"):
        for out, grad in zip((o_q, o_k, o_v), backs):
            out[...] = dot(tokens, grad, 1, 1, HI) / everyone
    with jax.named_scope("suma_high"):
        wait(7, ra3.at[pl.ds(0, NZH - 1)])
        ra4[xy] = jnp.sum(ra3[...], axis=0) / everyone
        send_all(8, plane, NXY - 1, lambda i: ra4.at[xy], ra4.at[xy])
    with jax.named_scope("out_last"):
        wait(17, rp4.at[pl.ds(0, NXY - 1)])
        o_out[...] = rp4[...].reshape(WIDTH, 128).T
    with jax.named_scope("sumb_back"):
        wait(11, rb2.at[pl.ds(0, NZ - 1)])
        rb3[xy] = jnp.sum(rb2[...], axis=0) / everyone
        send_all(12, plane, NXY - 1, lambda i: rb3.at[xy], rb3.at[xy])
    with jax.named_scope("small_back"):
        wait(19, rs2.at[pl.ds(0, NZ - 1)])
        rs3[xy] = jnp.sum(rs2[...], axis=0) / everyone
        send_all(20, plane, NXY - 1, lambda i: rs3.at[xy], rs3.at[xy])
    with jax.named_scope("suma_last"):
        wait(8, ra4.at[pl.ds(0, NXY - 1)])
        unpack(ra4, o_feat)
    with jax.named_scope("small_last"):
        wait(20, rs3.at[pl.ds(0, NXY - 1)])
        small = [rs3[k // ROWS3, k % ROWS3 : k % ROWS3 + 1, :] for k in range(SMALL)]
        for l in range(2):
            o_gain[:, 128 * l : 128 * l + 128] = small[l]
            o_bias[:, 128 * l : 128 * l + 128] = small[2 + l]
        folded = jnp.concatenate(small[8:], axis=0)
        o_slice[...] = (folded + pltpu.roll(folded, SLICES, 1))[:, :SLICES]
        lane, place = iota((1, 128), 1), iota((1, HEADS), 1)
        d_temper = jnp.zeros((1, HEADS), F32)
        for g in range(4):
            for s in range(2):
                part = jnp.where(lane // SLICES == s, small[4 + g], 0.0)
                part = jnp.sum(part, axis=1, keepdims=True)
                d_temper = jnp.where(place == 2 * g + s, part, d_temper)
        o_temper[...] = -d_temper / temper[...]
    with jax.named_scope("sumb_last"):
        wait(12, rb3.at[pl.ds(0, NXY - 1)])
        unpack(rb3, o_mid)

    with jax.named_scope("done"):
        for copy in unsent:
            copy.wait_send()


def hand_on(count, *refs):
    sems = refs[2 * count]
    copies = [pltpu.make_async_copy(refs[n], refs[count + n], sems.at[n]) for n in range(count)]
    for copy in copies:
        copy.start()
    for copy in copies:
        copy.wait()


def shards(
    points, out_grad, ln_gain, ln_bias, w_mid, w_feat, w_slice, temper, wq, wk, wv, w_out
):
    rows = points.shape[0]
    everyone = rows * NXY * NZ * NC
    hbm = pl.BlockSpec(memory_space=pltpu.HBM)
    vmem = pl.BlockSpec(memory_space=pltpu.VMEM)
    f = lambda *s: jax.ShapeDtypeStruct(s, F32)
    args = (
        points,
        out_grad,
        ln_gain.reshape(1, -1),
        ln_bias.reshape(1, -1),
        w_mid,
        w_feat,
        w_slice,
        temper.reshape(1, -1),
        wq,
        wk,
        wv,
        w_out,
    )
    out_shape = (
        jax.ShapeDtypeStruct((rows, WIDTH), BF16),
        f(1, WIDTH),
        f(1, WIDTH),
        f(128, WIDTH),
        f(128, WIDTH),
        f(DIM, SLICES),
        f(1, HEADS),
        f(DIM, DIM),
        f(DIM, DIM),
        f(DIM, DIM),
        f(128, WIDTH),
    )
    outs = pl.pallas_call(
        functools.partial(kernel, float(everyone), 128),
        out_shape=out_shape,
        in_specs=[hbm] * 12,
        out_specs=(vmem,) * 11,
        scratch_shapes=[pltpu.VMEM(a.shape, a.dtype) for a in args]
        + [pltpu.SemaphoreType.DMA((12,))]
        + [
            pltpu.VMEM((rows, WIDTH), F32),
            pltpu.VMEM((rows, 128), F32),
            pltpu.VMEM((rows, WIDTH), BF16),
            pltpu.VMEM((rows, WIDTH), BF16),
            pltpu.VMEM((rows, 2 * WIDTH), BF16),
            pltpu.VMEM((rows, WIDTH), BF16),
            pltpu.VMEM((rows, COLS), F32),
            pltpu.VMEM((rows, COLS), F32),
            pltpu.VMEM((rows, COLS), BF16),
            pltpu.VMEM((rows, COLS), BF16),
            pltpu.VMEM((rows, 2 * WIDTH), BF16),
            pltpu.VMEM((rows, WIDTH), F32),
        ]
        + [
            pltpu.VMEM(lead + (ROWS1, 128), F32)
            for lead in ((NC, NXY), (NC * NXY,), (NZ,), (NC * NXY,))
        ]
        + [
            pltpu.VMEM(lead + (16, 128), F32)
            for lead in ((NC, NXY), (NXY,), (NXY,), (NXY,), (LOW,), (NZH,), (NXY,))
        ]
        + [
            pltpu.VMEM(lead + (ROWS2, 128), F32)
            for lead in ((NC, NXY), (NXY,), (NXY,), (NXY,), (NZ,), (NXY,))
        ]
        + [
            pltpu.VMEM((NC, NXY, 16, WIDTH), F32),
            pltpu.VMEM((NXY, 16, WIDTH), F32),
            pltpu.VMEM((NXY, 16, WIDTH), F32),
            pltpu.VMEM((NXY, 16, WIDTH), F32),
            pltpu.VMEM((NZ, 1, WIDTH), F32),
            pltpu.VMEM((NZ, 1, WIDTH), F32),
            pltpu.VMEM((NZ, 1, 128), F32),
            pltpu.VMEM((NXY, 16, 128), F32),
            pltpu.VMEM((NC, 128, WIDTH), BF16),
        ]
        + [
            pltpu.VMEM((lead, ROWS3, 128), F32)
            for lead in (NXY, NXY, NXY, NXY, NZ, NXY)
        ]
        + [pltpu.SemaphoreType.DMA((21,)), pltpu.SemaphoreType.DMA((21,))],
        compiler_params=pltpu.CompilerParams(
            collective_id=0, has_side_effects=True, vmem_limit_bytes=VMEM_BYTES
        ),
        name="backward",
    )(*[pltpu.with_memory_space_constraint(a, pltpu.HBM) for a in args])
    outs = pl.pallas_call(
        functools.partial(hand_on, len(outs)),
        out_shape=out_shape,
        in_specs=[vmem] * 11,
        out_specs=(hbm,) * 11,
        scratch_shapes=[pltpu.SemaphoreType.DMA((11,))],
        name="hand_on",
    )(*[pltpu.with_memory_space_constraint(o, pltpu.VMEM) for o in outs])
    outs = list(outs)
    for n in (1, 2, 6):
        outs[n] = outs[n].reshape(-1)
    return tuple(outs)


def solution(mesh):
    by_point, by_rep = P(("pts", "rep"), None), P("rep", None)
    in_specs = (by_point, by_point) + (P(),) * 10
    out_specs = (by_point, P(), P(), by_rep, by_rep, P(), P(), P(), P(), P(), by_rep)
    return jax.shard_map(shards, mesh=mesh, in_specs=in_specs, out_specs=out_specs, check_vma=False)
```

```python
import functools

import jax
import jax.numpy as jnp
from jax import lax
from jax.experimental import pallas as pl
from jax.experimental.pallas import tpu as pltpu
from jax.sharding import PartitionSpec as P

MESH = pl.DeviceIdType.MESH
F32, BF16 = jnp.float32, jnp.bfloat16
HI = lax.Precision.HIGHEST

HEADS, SLICES, DIM = 8, 64, 32
WIDTH = HEADS * DIM
COLS = HEADS * SLICES
NX, NY, NZ, NC = 4, 4, 16, 2
NXY = NX * NY
ROWS1, ROWS2, ROWS3 = 9, 16, 3
SMALL = 40
VMEM_BYTES = 48 * 1024 * 1024
BF_MAX = 3.3895314e38


def dot(a, b, ca=1, cb=0, precision=None):
    return lax.dot_general(
        a, b, (((ca,), (cb,)), ((), ())), preferred_element_type=F32, precision=precision
    )


def iota(shape, dim):
    return lax.broadcasted_iota(jnp.int32, shape, dim)


def split(values):
    high = values.astype(BF16)
    return high, (values - high.astype(F32)).astype(BF16)


def group_sum(high, low, ones):
    parts = []
    for g in range(0, COLS, 256):
        parts.append(dot(high[:, g : g + 256], ones) + dot(low[:, g : g + 256], ones))
    return jnp.concatenate(parts, axis=1)


def block_diagonal(tile_t):
    whole = jnp.concatenate([tile_t] * HEADS, axis=0)
    own = iota((WIDTH, COLS), 0) // DIM == iota((WIDTH, COLS), 1) // SLICES
    return jnp.where(own, whole, 0.0)


def diagonal_rows(full):
    left = iota((DIM, 128), 1) < SLICES
    parts = []
    for g in range(HEADS // 2):
        cols = slice(128 * g, 128 * g + 128)
        parts.append(
            jnp.where(
                left,
                full[2 * DIM * g : 2 * DIM * g + DIM, cols],
                full[2 * DIM * g + DIM : 2 * DIM * g + 2 * DIM, cols],
            )
        )
    return parts


def thirds(values):
    first = values.astype(BF16)
    rest = values - first.astype(F32)
    second = rest.astype(BF16)
    return first, second, (rest - second.astype(F32)).astype(BF16)


def left_terms(parts, axis=0):
    a, b, c = parts
    return jnp.concatenate([a, a, b, a, b, c], axis=axis)


def right_terms(parts, axis=0):
    a, b, c = parts
    return jnp.concatenate([a, b, a, c, b, a], axis=axis)


def weight_terms(weights):
    terms = [part.astype(F32) for part in thirds(weights)]
    return left_terms(terms, 1).astype(BF16)


def pair_dot(left, right, cb):
    a, b = split(left)
    c, d = split(right)
    return dot(jnp.concatenate([a, a, b], axis=1), jnp.concatenate([c, d, c], axis=cb), 1, cb)


def token_step(totals, masses, d_mixed, forward_terms, backward_terms):
    scale = DIM ** (-0.5)
    inv = 1.0 / (masses + 1e-05)
    tokens = totals * inv
    qkv = dot(forward_terms, right_terms(thirds(tokens)))
    q, k, v = qkv[:DIM], qkv[DIM : 2 * DIM], qkv[2 * DIM :]
    q_terms, k_terms = left_terms(thirds(q)), right_terms(thirds(k))
    m_terms, v_terms = left_terms(thirds(d_mixed)), right_terms(thirds(v))
    same = iota((128, 128), 0) // SLICES == iota((128, 128), 1) // SLICES
    mixed, dq, dk, dv = [], [], [], []
    for g in range(HEADS // 2):
        cols = slice(128 * g, 128 * g + 128)
        scores = dot(q_terms[:, cols], k_terms[:, cols], 0, 0) * scale
        d_att = dot(m_terms[:, cols], v_terms[:, cols], 0, 0)
        powers = jnp.where(same, jnp.exp(scores), 0.0)
        att = powers / jnp.sum(powers, axis=1, keepdims=True)
        d_scores = att * (d_att - jnp.sum(d_att * att, axis=1, keepdims=True)) * scale
        mixed.append(pair_dot(v[:, cols], att, 1))
        dq.append(pair_dot(k[:, cols], d_scores, 1))
        dk.append(pair_dot(q[:, cols], d_scores, 0))
        dv.append(pair_dot(d_mixed[:, cols], att, 0))
    mixed = jnp.concatenate(mixed, axis=1)
    backs = [jnp.concatenate(d, axis=1) for d in (dq, dk, dv)]
    d_tokens = dot(
        backward_terms, jnp.concatenate([right_terms(thirds(d)) for d in backs], axis=0)
    )
    d_masses = -jnp.sum(d_tokens * tokens, axis=0, keepdims=True) * inv
    return mixed, d_tokens * inv, d_masses, tokens, backs


def far_first(a):
    return (2 - a + 3 * (a // 2) - 2 * (a // 3)) % 4


def kernel(
    everyone,
    chunk,
    points_h,
    out_grad_h,
    gain_h,
    bias_h,
    w_mid_h,
    w_feat_h,
    w_slice_h,
    temper_h,
    wq_h,
    wk_h,
    wv_h,
    w_out_h,
    o_points,
    o_gain,
    o_bias,
    o_mid,
    o_feat,
    o_slice,
    o_temper,
    o_q,
    o_k,
    o_v,
    o_out,
    points,
    out_grad,
    gain_ref,
    bias_ref,
    w_mid,
    w_feat,
    w_slice,
    temper,
    wq,
    wk,
    wv,
    w_out,
    loads,
    xhat_s,
    rstd_s,
    normed_s,
    mid_s,
    fd_s,
    low_s,
    logits_s,
    w_s,
    sw_s,
    sc_s,
    dmf_s,
    dn_s,
    p1,
    r11,
    r12,
    r13,
    pb,
    rb0,
    ab,
    rb1,
    rb2,
    rb3,
    pp,
    rp0,
    ap,
    rp1,
    sp,
    rp2,
    rp3,
    rp4,
    mb_s,
    tb_s,
    ps,
    rs0,
    as_,
    rs1,
    rs2,
    rs3,
    sends,
    recvs,
):
    held = (
        (points_h, points),
        (w_mid_h, w_mid),
        (w_feat_h, w_feat),
        (gain_h, gain_ref),
        (bias_h, bias_ref),
        (w_slice_h, w_slice),
        (temper_h, temper),
        (out_grad_h, out_grad),
        (w_out_h, w_out),
        (wq_h, wq),
        (wk_h, wk),
        (wv_h, wv),
    )
    copies = [pltpu.make_async_copy(a, b, loads.at[n]) for n, (a, b) in enumerate(held)]
    for copy in copies:
        copy.start()

    p, c = lax.axis_index("pts"), lax.axis_index("rep")
    x, y, z = p // (NY * NZ), p // NZ % NY, p % NZ
    xy = x * NY + y
    rows = points.shape[0]

    def plane_index(i):
        return (x + far_first(i // 4)) % NX * NY + (y + far_first(i % 4)) % NY

    def plane(i):
        return (plane_index(i) * NZ + z, c)

    def plane_cores(i):
        return (plane_index(i // 2) * NZ + z, (c + 1 + i % 2) % NC)

    def column_index(i):
        return (z + 8 + (i + 1) // 2 * (1 - 2 * (i % 2))) % NZ

    def column(i):
        return (xy * NZ + column_index(i), c)

    sibling = (p, 1 - c)
    barrier = pltpu.get_barrier_semaphore()

    greetings = [(plane_cores, i) for i in range(2 * NXY - 1)]
    greetings += [(column, i) for i in range(NZ - 1)]
    n_greetings = len(greetings)

    def greet(count):
        for who, i in greetings[:count]:
            pl.semaphore_signal(barrier, inc=1, device_id=who(i), device_id_type=MESH)
        del greetings[:count]

    with jax.named_scope("greet"):
        greet(n_greetings)

    unsent = []

    def pack(ref, grad):
        for h in range(NC):
            for l in range(2):
                ref[h, 8 * l : 8 * l + 8, 0:16, :] = grad[
                    128 * h : 128 * h + 128, 128 * l : 128 * l + 128
                ].reshape(8, 16, 128)

    def unpack(ref, out):
        for l in range(2):
            out[:, 128 * l : 128 * l + 128] = ref[8 * l : 8 * l + 8, 0:16, :].reshape(128, 128)

    def send_all(stage, who, count, src, dst):
        def body(i, _):
            pltpu.make_async_remote_copy(
                src(i), dst, sends.at[stage], recvs.at[stage], device_id=who(i), device_id_type=MESH
            ).start()
            return 0

        lax.fori_loop(0, count, body, 0)

    def swap(stage, src, dst):
        send_all(stage, lambda i: sibling, 1, lambda i: src, dst)

    def wait(stage, ref):
        copy = pltpu.make_async_remote_copy(
            ref, ref, sends.at[stage], recvs.at[stage], device_id=sibling, device_id_type=MESH
        )
        copy.wait_recv()
        unsent.append(copy)

    ones = (iota((256, 256), 0) // SLICES == iota((256, 256), 1) // SLICES).astype(F32).astype(BF16)

    with jax.named_scope("load"):
        for copy in copies[:7]:
            copy.wait()
    gain, bias = gain_ref[...], bias_ref[...]
    head_of = iota((1, COLS), 1) // SLICES
    temper_row = jnp.zeros((1, COLS), F32)
    for h in range(HEADS):
        temper_row = jnp.where(head_of == h, temper[:, h : h + 1], temper_row)
    inv_t = 1.0 / temper_row
    ws = w_slice[...].astype(F32)
    slice_blocks = block_diagonal(jnp.concatenate([ws] * HEADS, axis=1)).astype(BF16)

    with jax.named_scope("front"):
        for r in range(0, rows, chunk):
            here = pl.ds(r, chunk)
            xs = points[here, :].astype(F32)
            center = xs - jnp.mean(xs, axis=1, keepdims=True)
            rstd = lax.rsqrt(jnp.mean(center * center, axis=1, keepdims=True) + 1e-05)
            xhat = center * rstd
            xhat_s[here, :] = xhat
            rstd_s[here, :] = jnp.broadcast_to(rstd, (chunk, 128))
            normed = (xhat * gain + bias).astype(BF16)
            normed_s[here, :] = normed
            mid = dot(normed, w_mid[...]).astype(BF16)
            mid_s[here, :] = mid
            fd_s[here, WIDTH:] = dot(normed, w_feat[...]).astype(BF16)
            logits = dot(mid, slice_blocks) * inv_t
            logits_s[here, :] = logits
            powers = jnp.exp(logits)
            high = jnp.minimum(powers, BF_MAX).astype(BF16)
            low = (powers - high.astype(F32)).astype(BF16)
            weights = powers / group_sum(high, low, ones)
            w_s[here, :] = weights
            sw_s[here, :] = weights.astype(BF16)
        for copy in copies[7:]:
            copy.wait()
        for r in range(0, rows, chunk):
            here = pl.ds(r, chunk)
            d_high, d_low = split(dot(out_grad[here, :], w_out[...], 1, 1))
            fd_s[here, :WIDTH] = d_high
            low_s[here, :] = d_low

    with jax.named_scope("shares1"):
        sw = sw_s[...]
        by_fd = dot(fd_s[...], sw, 0, 0)
        by_low = dot(low_s[...], sw, 0, 0)
        tot = diagonal_rows(by_fd[WIDTH:])
        dmx = diagonal_rows(by_fd[:WIDTH] + by_low)
        mass = dot(jnp.ones((8, rows), BF16), sw)[:1]
        quarter = iota((1, 128), 1) // DIM
        for i in range(4):
            for j in range(4):
                k = 4 * i + j
                p1[0, k, 0:8, :] = tot[j][8 * i : 8 * i + 8]
                p1[1, k, 0:8, :] = dmx[j][8 * i : 8 * i + 8]
                p1[0, k, 8:9, :] = jnp.where(quarter == i, mass[:, 128 * j : 128 * j + 128], 0.0)
                p1[1, k, 8:9, :] = jnp.zeros((1, 128), F32)

    with jax.named_scope("barrier"):
        pl.semaphore_wait(barrier, n_greetings)

    me1 = c * NXY + xy
    with jax.named_scope("sum1_plane"):
        send_all(
            1,
            plane_cores,
            2 * NXY - 1,
            lambda i: p1.at[(c + 1 + i % 2) % NC, plane_index(i // 2)],
            r11.at[me1],
        )
        r11[me1] = p1[c, xy]
        projected = dot(out_grad[...], sw, 0, 0)
        by_normed = dot(normed_s[...], sw, 0, 0)
        for h in range(NC):
            half = projected[:, WIDTH * h : WIDTH * h + WIDTH]
            pp[h, :, 0:16, :] = half.reshape(NXY, 16, WIDTH)
            for l in range(2):
                half = by_normed[128 * h : 128 * h + 128, WIDTH * l : WIDTH * l + WIDTH]
                pp[h, :, 16 + 8 * l : 24 + 8 * l, :] = half.reshape(NXY, 8, WIDTH)
        swap(13, pp.at[1 - c], rp0)
        token_weights = (wq[...], wk[...], wv[...])
        forward_terms = jnp.concatenate([weight_terms(w.T) for w in token_weights], axis=0)
        backward_terms = jnp.concatenate([weight_terms(w) for w in token_weights], axis=1)
        wait(1, r11.at[pl.ds(0, 2 * NXY - 1)])
        r12[z] = jnp.sum(r11[...], axis=0)
    with jax.named_scope("sum1_column"):
        send_all(2, column, NZ - 1, lambda i: r12.at[z], r12.at[z])
        wait(13, rp0)
        ap[...] = pp[c] + rp0[...]
        send_all(14, plane, NXY - 1, lambda i: ap.at[plane_index(i)], rp1.at[xy])
        rp1[xy] = ap[xy]
        wait(2, r12.at[pl.ds(0, NZ - 1)])
        r13[me1] = jnp.sum(r12[...], axis=0)
    with jax.named_scope("sum1_back"):
        send_all(3, plane_cores, 2 * NXY - 1, lambda i: r13.at[me1], r13.at[me1])
        wait(14, rp1.at[pl.ds(0, NXY - 1)])
        piece = jnp.sum(rp1[...], axis=0)
        for k in range(NZ):
            sp[k, 0:1] = piece[k : k + 1]
            sp[k, 1:2] = piece[16 + k : 17 + k]
        send_all(15, column, NZ - 1, lambda i: sp.at[column_index(i)], rp2.at[z])
        rp2[z] = sp[z]
        wait(3, r13.at[pl.ds(0, 2 * NXY - 1)])

    def whole(half):
        return jnp.concatenate(
            [
                jnp.concatenate([r13[NXY * half + 4 * i + j, 0:8, :] for i in range(4)], axis=0)
                for j in range(4)
            ],
            axis=1,
        )

    with jax.named_scope("tokens"):
        masses = jnp.concatenate(
            [sum(r13[4 * i + j, 8:9, :] for i in range(4)) for j in range(4)], axis=1
        )
        mixed, d_totals, d_masses, tokens, backs = token_step(
            whole(0), masses, whole(1), forward_terms, backward_terms
        )
        mixed_blocks = block_diagonal(mixed.astype(BF16).astype(F32)).astype(BF16)
        totals_blocks = block_diagonal(d_totals.astype(BF16).astype(F32)).astype(BF16)
        both = jnp.concatenate([mixed_blocks, totals_blocks], axis=0)
        for h in range(NC):
            part = (slice(128 * h, 128 * h + 128), slice(WIDTH * h, WIDTH * h + WIDTH))
            mb_s[h] = mixed_blocks[part]
            tb_s[h] = totals_blocks[part]

    w_both = jnp.concatenate([w_mid[...], w_feat[...]], axis=1)

    def fold(values):
        return jnp.sum(values.reshape(values.shape[0] // 8, 8, values.shape[1]), axis=0)

    sums = [jnp.zeros((8, COLS), F32), jnp.zeros((8, WIDTH), F32), jnp.zeros((8, WIDTH), F32)]

    def back(r):
        here = pl.ds(r, chunk)
        weights = w_s[here, :]
        d_weights = dot(fd_s[here, :], both) + d_masses
        high, low = split(d_weights * weights)
        d_logits = weights * (d_weights - group_sum(high, low, ones))
        scaled = (d_logits * inv_t).astype(BF16)
        sc_s[here, :] = scaled
        sums[0] += fold(d_logits * logits_s[here, :])
        dmf_s[here, :WIDTH] = dot(scaled, slice_blocks, 1, 1).astype(BF16)

    def norm(r):
        here = pl.ds(r, chunk)
        dmf_s[here, WIDTH:] = dot(sw_s[here, :], totals_blocks, 1, 1).astype(BF16)
        d_normed = dot(dmf_s[here, :], w_both, 1, 1)
        dn_s[here, :] = d_normed
        sums[1] += fold(d_normed * xhat_s[here, :])
        sums[2] += fold(d_normed)

    with jax.named_scope("back"):
        for r in range(0, rows, chunk):
            back(r)
    with jax.named_scope("sumb_core"):
        pack(pb, dot(normed_s[...], dmf_s[:, :WIDTH], 0, 0))
        swap(9, pb.at[1 - c], rb0)
        for r in range(0, rows // 2, chunk):
            norm(r)
    with jax.named_scope("sumb_plane"):
        wait(9, rb0)
        ab[...] = pb[c] + rb0[...]
        send_all(10, plane, NXY - 1, lambda i: ab.at[plane_index(i)], rb1.at[xy])
        rb1[xy] = ab[xy]
    with jax.named_scope("shares_small"):
        for r in range(rows // 2, rows, chunk):
            norm(r)
        slice_sum = sum(diagonal_rows(dot(mid_s[...], sc_s[...], 0, 0)))
        temper_sum, gain_sum, bias_sum = (jnp.sum(v, axis=0, keepdims=True) for v in sums)
        small = [gain_sum[:, 128 * l : 128 * l + 128] for l in range(2)]
        small += [bias_sum[:, 128 * l : 128 * l + 128] for l in range(2)]
        small += [temper_sum[:, 128 * l : 128 * l + 128] for l in range(4)]
        small += [slice_sum, jnp.zeros((ROWS3 * NXY - SMALL, 128), F32)]
        small = jnp.concatenate(small, axis=0)
        for k in range(NXY):
            ps[k] = small[ROWS3 * k : ROWS3 * k + ROWS3]
        swap(0, ps, rs0)

    with jax.named_scope("out_feat"):
        wait(15, rp2.at[pl.ds(0, NZ - 1)])
        summed = jnp.sum(rp2[...], axis=0)
        for n, blocks in enumerate((mb_s[c], tb_s[z // 8])):
            row_high, row_low = split(jnp.broadcast_to(summed[n : n + 1], (16, WIDTH)))
            own = dot(row_high, blocks, 1, 1) + dot(row_low, blocks, 1, 1)
            rp3[z, n : n + 1] = own[:1] / everyone
        send_all(16, column, NZ - 1, lambda i: rp3.at[z], rp3.at[z])

    with jax.named_scope("small_plane"):
        wait(0, rs0)
        as_[...] = ps[...] + rs0[...]
        send_all(18, plane, NXY - 1, lambda i: as_.at[plane_index(i)], rs1.at[xy])
        rs1[xy] = as_[xy]
    with jax.named_scope("points"):
        for r in range(0, rows, chunk):
            here = pl.ds(r, chunk)
            xhat = xhat_s[here, :]
            d_xhat = dn_s[here, :] * gain
            inner = d_xhat - jnp.mean(d_xhat, axis=1, keepdims=True)
            inner = inner - xhat * jnp.mean(d_xhat * xhat, axis=1, keepdims=True)
            o_points[here, :] = (inner * rstd_s[here, 0:1]).astype(BF16)

    with jax.named_scope("sumb_column"):
        wait(10, rb1.at[pl.ds(0, NXY - 1)])
        rb2[z] = jnp.sum(rb1[...], axis=0)
        send_all(11, column, NZ - 1, lambda i: rb2.at[z], rb2.at[z])
    with jax.named_scope("small_column"):
        wait(18, rs1.at[pl.ds(0, NXY - 1)])
        rs2[z] = jnp.sum(rs1[...], axis=0)
        send_all(19, column, NZ - 1, lambda i: rs2.at[z], rs2.at[z])
    with jax.named_scope("out_column"):
        wait(16, rp3.at[pl.ds(0, NZ - 1)])
        for n in range(2):
            rp4[xy, n] = jnp.concatenate([rp3[k, n : n + 1] for k in range(NZ)], axis=0)
        send_all(17, plane, NXY - 1, lambda i: rp4.at[xy], rp4.at[xy])
    with jax.named_scope("token_grads"):
        for out, grad in zip((o_q, o_k, o_v), backs):
            out[...] = dot(tokens, grad, 1, 1, HI) / everyone
    with jax.named_scope("out_last"):
        wait(17, rp4.at[pl.ds(0, NXY - 1)])
        o_out[...] = rp4[:, 0].reshape(WIDTH, 128).T
        for l in range(2):
            o_feat[:, 128 * l : 128 * l + 128] = rp4[:, 1, 8 * l : 8 * l + 8, :].reshape(128, 128)
    with jax.named_scope("sumb_back"):
        wait(11, rb2.at[pl.ds(0, NZ - 1)])
        rb3[xy] = jnp.sum(rb2[...], axis=0) / everyone
        send_all(12, plane, NXY - 1, lambda i: rb3.at[xy], rb3.at[xy])
    with jax.named_scope("small_back"):
        wait(19, rs2.at[pl.ds(0, NZ - 1)])
        rs3[xy] = jnp.sum(rs2[...], axis=0) / everyone
        send_all(20, plane, NXY - 1, lambda i: rs3.at[xy], rs3.at[xy])
    with jax.named_scope("small_last"):
        wait(20, rs3.at[pl.ds(0, NXY - 1)])
        small = [rs3[k // ROWS3, k % ROWS3 : k % ROWS3 + 1, :] for k in range(SMALL)]
        for l in range(2):
            o_gain[:, 128 * l : 128 * l + 128] = small[l]
            o_bias[:, 128 * l : 128 * l + 128] = small[2 + l]
        folded = jnp.concatenate(small[8:], axis=0)
        o_slice[...] = (folded + pltpu.roll(folded, SLICES, 1))[:, :SLICES]
        lane, place = iota((1, 128), 1), iota((1, HEADS), 1)
        d_temper = jnp.zeros((1, HEADS), F32)
        for g in range(4):
            for s in range(2):
                part = jnp.where(lane // SLICES == s, small[4 + g], 0.0)
                part = jnp.sum(part, axis=1, keepdims=True)
                d_temper = jnp.where(place == 2 * g + s, part, d_temper)
        o_temper[...] = -d_temper / temper[...]
    with jax.named_scope("sumb_last"):
        wait(12, rb3.at[pl.ds(0, NXY - 1)])
        unpack(rb3, o_mid)

    with jax.named_scope("done"):
        for copy in unsent:
            copy.wait_send()


def hand_on(count, *refs):
    sems = refs[2 * count]
    copies = [pltpu.make_async_copy(refs[n], refs[count + n], sems.at[n]) for n in range(count)]
    for copy in copies:
        copy.start()
    for copy in copies:
        copy.wait()


def shards(
    points, out_grad, ln_gain, ln_bias, w_mid, w_feat, w_slice, temper, wq, wk, wv, w_out
):
    rows = points.shape[0]
    everyone = rows * NXY * NZ * NC
    hbm = pl.BlockSpec(memory_space=pltpu.HBM)
    vmem = pl.BlockSpec(memory_space=pltpu.VMEM)
    f = lambda *s: jax.ShapeDtypeStruct(s, F32)
    args = (
        points,
        out_grad,
        ln_gain.reshape(1, -1),
        ln_bias.reshape(1, -1),
        w_mid,
        w_feat,
        w_slice,
        temper.reshape(1, -1),
        wq,
        wk,
        wv,
        w_out,
    )
    out_shape = (
        jax.ShapeDtypeStruct((rows, WIDTH), BF16),
        f(1, WIDTH),
        f(1, WIDTH),
        f(128, WIDTH),
        f(128, WIDTH),
        f(DIM, SLICES),
        f(1, HEADS),
        f(DIM, DIM),
        f(DIM, DIM),
        f(DIM, DIM),
        f(128, WIDTH),
    )
    outs = pl.pallas_call(
        functools.partial(kernel, float(everyone), 256),
        out_shape=out_shape,
        in_specs=[hbm] * 12,
        out_specs=(vmem,) * 11,
        scratch_shapes=[pltpu.VMEM(a.shape, a.dtype) for a in args]
        + [pltpu.SemaphoreType.DMA((12,))]
        + [
            pltpu.VMEM((rows, WIDTH), F32),
            pltpu.VMEM((rows, 128), F32),
            pltpu.VMEM((rows, WIDTH), BF16),
            pltpu.VMEM((rows, WIDTH), BF16),
            pltpu.VMEM((rows, 2 * WIDTH), BF16),
            pltpu.VMEM((rows, WIDTH), BF16),
            pltpu.VMEM((rows, COLS), F32),
            pltpu.VMEM((rows, COLS), F32),
            pltpu.VMEM((rows, COLS), BF16),
            pltpu.VMEM((rows, COLS), BF16),
            pltpu.VMEM((rows, 2 * WIDTH), BF16),
            pltpu.VMEM((rows, WIDTH), F32),
        ]
        + [
            pltpu.VMEM(lead + (ROWS1, 128), F32)
            for lead in ((NC, NXY), (NC * NXY,), (NZ,), (NC * NXY,))
        ]
        + [
            pltpu.VMEM(lead + (ROWS2, 128), F32)
            for lead in ((NC, NXY), (NXY,), (NXY,), (NXY,), (NZ,), (NXY,))
        ]
        + [
            pltpu.VMEM((NC, NXY, 32, WIDTH), F32),
            pltpu.VMEM((NXY, 32, WIDTH), F32),
            pltpu.VMEM((NXY, 32, WIDTH), F32),
            pltpu.VMEM((NXY, 32, WIDTH), F32),
            pltpu.VMEM((NZ, 2, WIDTH), F32),
            pltpu.VMEM((NZ, 2, WIDTH), F32),
            pltpu.VMEM((NZ, 2, 128), F32),
            pltpu.VMEM((NXY, 2, 16, 128), F32),
            pltpu.VMEM((NC, 128, WIDTH), BF16),
            pltpu.VMEM((NC, 128, WIDTH), BF16),
        ]
        + [
            pltpu.VMEM((lead, ROWS3, 128), F32)
            for lead in (NXY, NXY, NXY, NXY, NZ, NXY)
        ]
        + [pltpu.SemaphoreType.DMA((21,)), pltpu.SemaphoreType.DMA((21,))],
        compiler_params=pltpu.CompilerParams(
            collective_id=0, has_side_effects=True, vmem_limit_bytes=VMEM_BYTES
        ),
        name="backward",
    )(*[pltpu.with_memory_space_constraint(a, pltpu.HBM) for a in args])
    outs = pl.pallas_call(
        functools.partial(hand_on, len(outs)),
        out_shape=out_shape,
        in_specs=[vmem] * 11,
        out_specs=(hbm,) * 11,
        scratch_shapes=[pltpu.SemaphoreType.DMA((11,))],
        name="hand_on",
    )(*[pltpu.with_memory_space_constraint(o, pltpu.VMEM) for o in outs])
    outs = list(outs)
    for n in (1, 2, 6):
        outs[n] = outs[n].reshape(-1)
    return tuple(outs)


def solution(mesh):
    by_point, by_rep = P(("pts", "rep"), None), P("rep", None)
    in_specs = (by_point, by_point) + (P(),) * 10
    out_specs = (by_point, P(), P(), by_rep, by_rep, P(), P(), P(), P(), P(), by_rep)
    return jax.shard_map(shards, mesh=mesh, in_specs=in_specs, out_specs=out_specs, check_vma=False)
```

```python
import functools

import jax
import jax.numpy as jnp
from jax import lax
from jax.experimental import pallas as pl
from jax.experimental.pallas import tpu as pltpu
from jax.sharding import PartitionSpec as P

MESH = pl.DeviceIdType.MESH
F32, BF16 = jnp.float32, jnp.bfloat16
HI = lax.Precision.HIGHEST

HEADS, SLICES, DIM = 8, 64, 32
WIDTH = HEADS * DIM
COLS = HEADS * SLICES
NX, NY, NZ, NC = 4, 4, 16, 2
NXY = NX * NY
ROWS1, ROWS2, ROWS3 = 9, 16, 3
SMALL = 40
VMEM_BYTES = 48 * 1024 * 1024
BF_MAX = 3.3895314e38


def dot(a, b, ca=1, cb=0, precision=None):
    return lax.dot_general(
        a, b, (((ca,), (cb,)), ((), ())), preferred_element_type=F32, precision=precision
    )


def iota(shape, dim):
    return lax.broadcasted_iota(jnp.int32, shape, dim)


def split(values):
    high = values.astype(BF16)
    return high, (values - high.astype(F32)).astype(BF16)


def group_sum(high, low, ones):
    parts = []
    for g in range(0, COLS, 256):
        parts.append(dot(high[:, g : g + 256], ones) + dot(low[:, g : g + 256], ones))
    return jnp.concatenate(parts, axis=1)


def block_diagonal(tile_t):
    whole = jnp.concatenate([tile_t] * HEADS, axis=0)
    own = iota((WIDTH, COLS), 0) // DIM == iota((WIDTH, COLS), 1) // SLICES
    return jnp.where(own, whole, 0.0)


def diagonal_rows(full):
    left = iota((DIM, 128), 1) < SLICES
    parts = []
    for g in range(HEADS // 2):
        cols = slice(128 * g, 128 * g + 128)
        parts.append(
            jnp.where(
                left,
                full[2 * DIM * g : 2 * DIM * g + DIM, cols],
                full[2 * DIM * g + DIM : 2 * DIM * g + 2 * DIM, cols],
            )
        )
    return parts


def thirds(values):
    first = values.astype(BF16)
    rest = values - first.astype(F32)
    second = rest.astype(BF16)
    return first, second, (rest - second.astype(F32)).astype(BF16)


def left_terms(parts, axis=0):
    a, b, c = parts
    return jnp.concatenate([a, a, b, a, b, c], axis=axis)


def right_terms(parts, axis=0):
    a, b, c = parts
    return jnp.concatenate([a, b, a, c, b, a], axis=axis)


def weight_terms(weights):
    terms = [part.astype(F32) for part in thirds(weights)]
    return left_terms(terms, 1).astype(BF16)


def pair_dot(left, right, cb):
    a, b = split(left)
    c, d = split(right)
    return dot(jnp.concatenate([a, a, b], axis=1), jnp.concatenate([c, d, c], axis=cb), 1, cb)


def token_step(totals, masses, d_mixed, forward_terms, backward_terms):
    scale = DIM ** (-0.5)
    inv = 1.0 / (masses + 1e-05)
    tokens = totals * inv
    qkv = dot(forward_terms, right_terms(thirds(tokens)))
    q, k, v = qkv[:DIM], qkv[DIM : 2 * DIM], qkv[2 * DIM :]
    q_terms, k_terms = left_terms(thirds(q)), right_terms(thirds(k))
    m_terms, v_terms = left_terms(thirds(d_mixed)), right_terms(thirds(v))
    same = iota((128, 128), 0) // SLICES == iota((128, 128), 1) // SLICES
    mixed, dq, dk, dv = [], [], [], []
    for g in range(HEADS // 2):
        cols = slice(128 * g, 128 * g + 128)
        scores = dot(q_terms[:, cols], k_terms[:, cols], 0, 0) * scale
        d_att = dot(m_terms[:, cols], v_terms[:, cols], 0, 0)
        powers = jnp.where(same, jnp.exp(scores), 0.0)
        att = powers / jnp.sum(powers, axis=1, keepdims=True)
        d_scores = att * (d_att - jnp.sum(d_att * att, axis=1, keepdims=True)) * scale
        mixed.append(pair_dot(v[:, cols], att, 1))
        dq.append(pair_dot(k[:, cols], d_scores, 1))
        dk.append(pair_dot(q[:, cols], d_scores, 0))
        dv.append(pair_dot(d_mixed[:, cols], att, 0))
    mixed = jnp.concatenate(mixed, axis=1)
    backs = [jnp.concatenate(d, axis=1) for d in (dq, dk, dv)]
    d_tokens = dot(
        backward_terms, jnp.concatenate([right_terms(thirds(d)) for d in backs], axis=0)
    )
    d_masses = -jnp.sum(d_tokens * tokens, axis=0, keepdims=True) * inv
    return mixed, d_tokens * inv, d_masses, tokens, backs


def far_first(a):
    return (2 - a + 3 * (a // 2) - 2 * (a // 3)) % 4


def kernel(
    everyone,
    chunk,
    points_h,
    out_grad_h,
    gain_h,
    bias_h,
    w_mid_h,
    w_feat_h,
    w_slice_h,
    temper_h,
    wq_h,
    wk_h,
    wv_h,
    w_out_h,
    o_points,
    o_gain,
    o_bias,
    o_mid,
    o_feat,
    o_slice,
    o_temper,
    o_q,
    o_k,
    o_v,
    o_out,
    points,
    out_grad,
    gain_ref,
    bias_ref,
    w_mid,
    w_feat,
    w_slice,
    temper,
    wq,
    wk,
    wv,
    w_out,
    loads,
    xhat_s,
    rstd_s,
    normed_s,
    mid_s,
    fd_s,
    low_s,
    logits_s,
    w_s,
    sw_s,
    sc_s,
    dmf_s,
    dn_s,
    p1,
    r11,
    r12,
    r13,
    pb,
    rb0,
    ab,
    rb1,
    rb2,
    rb3,
    pp,
    rp0,
    ap,
    rp1,
    sp,
    rp2,
    rp3,
    rp4,
    mb_s,
    tb_s,
    ps,
    rs0,
    as_,
    rs1,
    rs2,
    rs3,
    sends,
    recvs,
):
    held = (
        (points_h, points),
        (w_mid_h, w_mid),
        (w_feat_h, w_feat),
        (gain_h, gain_ref),
        (bias_h, bias_ref),
        (w_slice_h, w_slice),
        (temper_h, temper),
        (out_grad_h, out_grad),
        (w_out_h, w_out),
        (wq_h, wq),
        (wk_h, wk),
        (wv_h, wv),
    )
    copies = [pltpu.make_async_copy(a, b, loads.at[n]) for n, (a, b) in enumerate(held)]
    for copy in copies:
        copy.start()

    p, c = lax.axis_index("pts"), lax.axis_index("rep")
    x, y, z = p // (NY * NZ), p // NZ % NY, p % NZ
    xy = x * NY + y
    rows = points.shape[0]

    def plane_index(i):
        return (x + far_first(i // 4)) % NX * NY + (y + far_first(i % 4)) % NY

    def plane(i):
        return (plane_index(i) * NZ + z, c)

    def plane_cores(i):
        return (plane_index(i // 2) * NZ + z, (c + 1 + i % 2) % NC)

    def column_index(i):
        return (z + 8 + (i + 1) // 2 * (1 - 2 * (i % 2))) % NZ

    def column(i):
        return (xy * NZ + column_index(i), c)

    sibling = (p, 1 - c)
    barrier = pltpu.get_barrier_semaphore()

    greetings = [(plane_cores, i) for i in range(2 * NXY - 1)]
    greetings += [(column, i) for i in range(NZ - 1)]
    n_greetings = len(greetings)

    def greet(count):
        for who, i in greetings[:count]:
            pl.semaphore_signal(barrier, inc=1, device_id=who(i), device_id_type=MESH)
        del greetings[:count]

    with jax.named_scope("greet"):
        greet(n_greetings)

    unsent = []

    def pack(ref, grad):
        for h in range(NC):
            for l in range(2):
                ref[h, 8 * l : 8 * l + 8, 0:16, :] = grad[
                    128 * h : 128 * h + 128, 128 * l : 128 * l + 128
                ].reshape(8, 16, 128)

    def unpack(ref, out):
        for l in range(2):
            out[:, 128 * l : 128 * l + 128] = ref[8 * l : 8 * l + 8, 0:16, :].reshape(128, 128)

    def send_all(stage, who, count, src, dst):
        def body(i, _):
            pltpu.make_async_remote_copy(
                src(i), dst, sends.at[stage], recvs.at[stage], device_id=who(i), device_id_type=MESH
            ).start()
            return 0

        if count < NXY:
            for i in range(count):
                body(i, 0)
        else:
            lax.fori_loop(0, count, body, 0)

    def swap(stage, src, dst):
        send_all(stage, lambda i: sibling, 1, lambda i: src, dst)

    def wait(stage, ref):
        copy = pltpu.make_async_remote_copy(
            ref, ref, sends.at[stage], recvs.at[stage], device_id=sibling, device_id_type=MESH
        )
        copy.wait_recv()
        unsent.append(copy)

    ones = (iota((256, 256), 0) // SLICES == iota((256, 256), 1) // SLICES).astype(F32).astype(BF16)

    with jax.named_scope("load"):
        for copy in copies[:7]:
            copy.wait()
    gain, bias = gain_ref[...], bias_ref[...]
    head_of = iota((1, COLS), 1) // SLICES
    temper_row = jnp.zeros((1, COLS), F32)
    for h in range(HEADS):
        temper_row = jnp.where(head_of == h, temper[:, h : h + 1], temper_row)
    inv_t = 1.0 / temper_row
    ws = w_slice[...].astype(F32)
    slice_blocks = block_diagonal(jnp.concatenate([ws] * HEADS, axis=1)).astype(BF16)

    with jax.named_scope("front"):
        for r in range(0, rows, chunk):
            here = pl.ds(r, chunk)
            xs = points[here, :].astype(F32)
            center = xs - jnp.mean(xs, axis=1, keepdims=True)
            rstd = lax.rsqrt(jnp.mean(center * center, axis=1, keepdims=True) + 1e-05)
            xhat = center * rstd
            xhat_s[here, :] = xhat
            rstd_s[here, :] = jnp.broadcast_to(rstd, (chunk, 128))
            normed = (xhat * gain + bias).astype(BF16)
            normed_s[here, :] = normed
            mid = dot(normed, w_mid[...]).astype(BF16)
            mid_s[here, :] = mid
            fd_s[here, WIDTH:] = dot(normed, w_feat[...]).astype(BF16)
            logits = dot(mid, slice_blocks) * inv_t
            logits_s[here, :] = logits
            powers = jnp.exp(logits)
            high = jnp.minimum(powers, BF_MAX).astype(BF16)
            low = (powers - high.astype(F32)).astype(BF16)
            weights = powers / group_sum(high, low, ones)
            w_s[here, :] = weights
            sw_s[here, :] = weights.astype(BF16)
        for copy in copies[7:]:
            copy.wait()
        for r in range(0, rows, chunk):
            here = pl.ds(r, chunk)
            d_high, d_low = split(dot(out_grad[here, :], w_out[...], 1, 1))
            fd_s[here, :WIDTH] = d_high
            low_s[here, :] = d_low

    with jax.named_scope("shares1"):
        sw = sw_s[...]
        by_fd = dot(fd_s[...], sw, 0, 0)
        by_low = dot(low_s[...], sw, 0, 0)
        tot = diagonal_rows(by_fd[WIDTH:])
        dmx = diagonal_rows(by_fd[:WIDTH] + by_low)
        mass = dot(jnp.ones((8, rows), BF16), sw)[:1]
        quarter = iota((1, 128), 1) // DIM
        for i in range(4):
            for j in range(4):
                k = 4 * i + j
                p1[0, k, 0:8, :] = tot[j][8 * i : 8 * i + 8]
                p1[1, k, 0:8, :] = dmx[j][8 * i : 8 * i + 8]
                p1[0, k, 8:9, :] = jnp.where(quarter == i, mass[:, 128 * j : 128 * j + 128], 0.0)
                p1[1, k, 8:9, :] = jnp.zeros((1, 128), F32)

    with jax.named_scope("barrier"):
        pl.semaphore_wait(barrier, n_greetings)

    me1 = c * NXY + xy
    with jax.named_scope("sum1_plane"):
        send_all(
            1,
            plane_cores,
            2 * NXY - 1,
            lambda i: p1.at[(c + 1 + i % 2) % NC, plane_index(i // 2)],
            r11.at[me1],
        )
        r11[me1] = p1[c, xy]
        projected = dot(out_grad[...], sw, 0, 0)
        by_normed = dot(normed_s[...], sw, 0, 0)
        for h in range(NC):
            half = projected[:, WIDTH * h : WIDTH * h + WIDTH]
            pp[h, :, 0:16, :] = half.reshape(NXY, 16, WIDTH)
            for l in range(2):
                half = by_normed[128 * h : 128 * h + 128, WIDTH * l : WIDTH * l + WIDTH]
                pp[h, :, 16 + 8 * l : 24 + 8 * l, :] = half.reshape(NXY, 8, WIDTH)
        swap(13, pp.at[1 - c], rp0)
        token_weights = (wq[...], wk[...], wv[...])
        forward_terms = jnp.concatenate([weight_terms(w.T) for w in token_weights], axis=0)
        backward_terms = jnp.concatenate([weight_terms(w) for w in token_weights], axis=1)
        wait(1, r11.at[pl.ds(0, 2 * NXY - 1)])
        r12[z] = jnp.sum(r11[...], axis=0)
    with jax.named_scope("sum1_column"):
        send_all(2, column, NZ - 1, lambda i: r12.at[z], r12.at[z])
        wait(13, rp0)
        ap[...] = pp[c] + rp0[...]
        send_all(14, plane, NXY - 1, lambda i: ap.at[plane_index(i)], rp1.at[xy])
        rp1[xy] = ap[xy]
        wait(2, r12.at[pl.ds(0, NZ - 1)])
        r13[me1] = jnp.sum(r12[...], axis=0)
    with jax.named_scope("sum1_back"):
        send_all(3, plane_cores, 2 * NXY - 1, lambda i: r13.at[me1], r13.at[me1])
        wait(14, rp1.at[pl.ds(0, NXY - 1)])
        piece = jnp.sum(rp1[...], axis=0)
        for k in range(NZ):
            sp[k, 0:1] = piece[k : k + 1]
            sp[k, 1:2] = piece[16 + k : 17 + k]
        send_all(15, column, NZ - 1, lambda i: sp.at[column_index(i)], rp2.at[z])
        rp2[z] = sp[z]
        wait(3, r13.at[pl.ds(0, 2 * NXY - 1)])

    def whole(half):
        return jnp.concatenate(
            [
                jnp.concatenate([r13[NXY * half + 4 * i + j, 0:8, :] for i in range(4)], axis=0)
                for j in range(4)
            ],
            axis=1,
        )

    with jax.named_scope("tokens"):
        masses = jnp.concatenate(
            [sum(r13[4 * i + j, 8:9, :] for i in range(4)) for j in range(4)], axis=1
        )
        mixed, d_totals, d_masses, tokens, backs = token_step(
            whole(0), masses, whole(1), forward_terms, backward_terms
        )
        mixed_blocks = block_diagonal(mixed.astype(BF16).astype(F32)).astype(BF16)
        totals_blocks = block_diagonal(d_totals.astype(BF16).astype(F32)).astype(BF16)
        both = jnp.concatenate([mixed_blocks, totals_blocks], axis=0)
        for h in range(NC):
            part = (slice(128 * h, 128 * h + 128), slice(WIDTH * h, WIDTH * h + WIDTH))
            mb_s[h] = mixed_blocks[part]
            tb_s[h] = totals_blocks[part]

    w_both = jnp.concatenate([w_mid[...], w_feat[...]], axis=1)

    def fold(values):
        return jnp.sum(values.reshape(values.shape[0] // 8, 8, values.shape[1]), axis=0)

    sums = [jnp.zeros((8, COLS), F32), jnp.zeros((8, WIDTH), F32), jnp.zeros((8, WIDTH), F32)]

    def back(r):
        here = pl.ds(r, chunk)
        weights = w_s[here, :]
        d_weights = dot(fd_s[here, :], both) + d_masses
        high, low = split(d_weights * weights)
        d_logits = weights * (d_weights - group_sum(high, low, ones))
        scaled = (d_logits * inv_t).astype(BF16)
        sc_s[here, :] = scaled
        sums[0] += fold(d_logits * logits_s[here, :])
        dmf_s[here, :WIDTH] = dot(scaled, slice_blocks, 1, 1).astype(BF16)

    def norm(r):
        here = pl.ds(r, chunk)
        dmf_s[here, WIDTH:] = dot(sw_s[here, :], totals_blocks, 1, 1).astype(BF16)
        d_normed = dot(dmf_s[here, :], w_both, 1, 1)
        dn_s[here, :] = d_normed
        sums[1] += fold(d_normed * xhat_s[here, :])
        sums[2] += fold(d_normed)

    with jax.named_scope("back"):
        for r in range(0, rows, chunk):
            back(r)
    with jax.named_scope("sumb_core"):
        pack(pb, dot(normed_s[...], dmf_s[:, :WIDTH], 0, 0))
        swap(9, pb.at[1 - c], rb0)
        for r in range(0, rows // 2, chunk):
            norm(r)
    with jax.named_scope("sumb_plane"):
        wait(9, rb0)
        ab[...] = pb[c] + rb0[...]
        send_all(10, plane, NXY - 1, lambda i: ab.at[plane_index(i)], rb1.at[xy])
        rb1[xy] = ab[xy]
    with jax.named_scope("shares_small"):
        for r in range(rows // 2, rows, chunk):
            norm(r)
        slice_sum = sum(diagonal_rows(dot(mid_s[...], sc_s[...], 0, 0)))
        temper_sum, gain_sum, bias_sum = (jnp.sum(v, axis=0, keepdims=True) for v in sums)
        small = [gain_sum[:, 128 * l : 128 * l + 128] for l in range(2)]
        small += [bias_sum[:, 128 * l : 128 * l + 128] for l in range(2)]
        small += [temper_sum[:, 128 * l : 128 * l + 128] for l in range(4)]
        small += [slice_sum, jnp.zeros((ROWS3 * NXY - SMALL, 128), F32)]
        small = jnp.concatenate(small, axis=0)
        for k in range(NXY):
            ps[k] = small[ROWS3 * k : ROWS3 * k + ROWS3]
        swap(0, ps, rs0)

    with jax.named_scope("out_feat"):
        wait(15, rp2.at[pl.ds(0, NZ - 1)])
        summed = jnp.sum(rp2[...], axis=0)
        for n, blocks in enumerate((mb_s[c], tb_s[z // 8])):
            row_high, row_low = split(jnp.broadcast_to(summed[n : n + 1], (16, WIDTH)))
            own = dot(row_high, blocks, 1, 1) + dot(row_low, blocks, 1, 1)
            rp3[z, n : n + 1] = own[:1] / everyone
        send_all(16, column, NZ - 1, lambda i: rp3.at[z], rp3.at[z])

    with jax.named_scope("small_plane"):
        wait(0, rs0)
        as_[...] = ps[...] + rs0[...]
        send_all(18, plane, NXY - 1, lambda i: as_.at[plane_index(i)], rs1.at[xy])
        rs1[xy] = as_[xy]
    with jax.named_scope("sumb_column"):
        wait(10, rb1.at[pl.ds(0, NXY - 1)])
        rb2[z] = jnp.sum(rb1[...], axis=0)
        send_all(11, column, NZ - 1, lambda i: rb2.at[z], rb2.at[z])
    with jax.named_scope("points"):
        for r in range(0, rows, chunk):
            here = pl.ds(r, chunk)
            xhat = xhat_s[here, :]
            d_xhat = dn_s[here, :] * gain
            inner = d_xhat - jnp.mean(d_xhat, axis=1, keepdims=True)
            inner = inner - xhat * jnp.mean(d_xhat * xhat, axis=1, keepdims=True)
            o_points[here, :] = (inner * rstd_s[here, 0:1]).astype(BF16)

    with jax.named_scope("small_column"):
        wait(18, rs1.at[pl.ds(0, NXY - 1)])
        rs2[z] = jnp.sum(rs1[...], axis=0)
        send_all(19, column, NZ - 1, lambda i: rs2.at[z], rs2.at[z])
    with jax.named_scope("out_column"):
        wait(16, rp3.at[pl.ds(0, NZ - 1)])
        for n in range(2):
            rp4[xy, n] = jnp.concatenate([rp3[k, n : n + 1] for k in range(NZ)], axis=0)
        send_all(17, plane, NXY - 1, lambda i: rp4.at[xy], rp4.at[xy])
    with jax.named_scope("token_grads"):
        for out, grad in zip((o_q, o_k, o_v), backs):
            out[...] = dot(tokens, grad, 1, 1, HI) / everyone
    with jax.named_scope("sumb_back"):
        wait(11, rb2.at[pl.ds(0, NZ - 1)])
        rb3[xy] = jnp.sum(rb2[...], axis=0) / everyone
        send_all(12, plane, NXY - 1, lambda i: rb3.at[xy], rb3.at[xy])
    with jax.named_scope("small_back"):
        wait(19, rs2.at[pl.ds(0, NZ - 1)])
        rs3[xy] = jnp.sum(rs2[...], axis=0) / everyone
        send_all(20, plane, NXY - 1, lambda i: rs3.at[xy], rs3.at[xy])
    with jax.named_scope("out_last"):
        wait(17, rp4.at[pl.ds(0, NXY - 1)])
        o_out[...] = rp4[:, 0].reshape(WIDTH, 128).T
        for l in range(2):
            o_feat[:, 128 * l : 128 * l + 128] = rp4[:, 1, 8 * l : 8 * l + 8, :].reshape(128, 128)
    with jax.named_scope("small_last"):
        wait(20, rs3.at[pl.ds(0, NXY - 1)])
        small = [rs3[k // ROWS3, k % ROWS3 : k % ROWS3 + 1, :] for k in range(SMALL)]
        for l in range(2):
            o_gain[:, 128 * l : 128 * l + 128] = small[l]
            o_bias[:, 128 * l : 128 * l + 128] = small[2 + l]
        folded = jnp.concatenate(small[8:], axis=0)
        o_slice[...] = (folded + pltpu.roll(folded, SLICES, 1))[:, :SLICES]
        lane, place = iota((1, 128), 1), iota((1, HEADS), 1)
        d_temper = jnp.zeros((1, HEADS), F32)
        for g in range(4):
            for s in range(2):
                part = jnp.where(lane // SLICES == s, small[4 + g], 0.0)
                part = jnp.sum(part, axis=1, keepdims=True)
                d_temper = jnp.where(place == 2 * g + s, part, d_temper)
        o_temper[...] = -d_temper / temper[...]
    with jax.named_scope("sumb_last"):
        wait(12, rb3.at[pl.ds(0, NXY - 1)])
        unpack(rb3, o_mid)

    with jax.named_scope("done"):
        for copy in unsent:
            copy.wait_send()


def hand_on(count, *refs):
    sems = refs[2 * count]
    copies = [pltpu.make_async_copy(refs[n], refs[count + n], sems.at[n]) for n in range(count)]
    for copy in copies:
        copy.start()
    for copy in copies:
        copy.wait()


def shards(
    points, out_grad, ln_gain, ln_bias, w_mid, w_feat, w_slice, temper, wq, wk, wv, w_out
):
    rows = points.shape[0]
    everyone = rows * NXY * NZ * NC
    hbm = pl.BlockSpec(memory_space=pltpu.HBM)
    vmem = pl.BlockSpec(memory_space=pltpu.VMEM)
    f = lambda *s: jax.ShapeDtypeStruct(s, F32)
    args = (
        points,
        out_grad,
        ln_gain.reshape(1, -1),
        ln_bias.reshape(1, -1),
        w_mid,
        w_feat,
        w_slice,
        temper.reshape(1, -1),
        wq,
        wk,
        wv,
        w_out,
    )
    out_shape = (
        jax.ShapeDtypeStruct((rows, WIDTH), BF16),
        f(1, WIDTH),
        f(1, WIDTH),
        f(128, WIDTH),
        f(128, WIDTH),
        f(DIM, SLICES),
        f(1, HEADS),
        f(DIM, DIM),
        f(DIM, DIM),
        f(DIM, DIM),
        f(128, WIDTH),
    )
    outs = pl.pallas_call(
        functools.partial(kernel, float(everyone), 256),
        out_shape=out_shape,
        in_specs=[hbm] * 12,
        out_specs=(vmem,) * 11,
        scratch_shapes=[pltpu.VMEM(a.shape, a.dtype) for a in args]
        + [pltpu.SemaphoreType.DMA((12,))]
        + [
            pltpu.VMEM((rows, WIDTH), F32),
            pltpu.VMEM((rows, 128), F32),
            pltpu.VMEM((rows, WIDTH), BF16),
            pltpu.VMEM((rows, WIDTH), BF16),
            pltpu.VMEM((rows, 2 * WIDTH), BF16),
            pltpu.VMEM((rows, WIDTH), BF16),
            pltpu.VMEM((rows, COLS), F32),
            pltpu.VMEM((rows, COLS), F32),
            pltpu.VMEM((rows, COLS), BF16),
            pltpu.VMEM((rows, COLS), BF16),
            pltpu.VMEM((rows, 2 * WIDTH), BF16),
            pltpu.VMEM((rows, WIDTH), F32),
        ]
        + [
            pltpu.VMEM(lead + (ROWS1, 128), F32)
            for lead in ((NC, NXY), (NC * NXY,), (NZ,), (NC * NXY,))
        ]
        + [
            pltpu.VMEM(lead + (ROWS2, 128), F32)
            for lead in ((NC, NXY), (NXY,), (NXY,), (NXY,), (NZ,), (NXY,))
        ]
        + [
            pltpu.VMEM((NC, NXY, 32, WIDTH), F32),
            pltpu.VMEM((NXY, 32, WIDTH), F32),
            pltpu.VMEM((NXY, 32, WIDTH), F32),
            pltpu.VMEM((NXY, 32, WIDTH), F32),
            pltpu.VMEM((NZ, 2, WIDTH), F32),
            pltpu.VMEM((NZ, 2, WIDTH), F32),
            pltpu.VMEM((NZ, 2, 128), F32),
            pltpu.VMEM((NXY, 2, 16, 128), F32),
            pltpu.VMEM((NC, 128, WIDTH), BF16),
            pltpu.VMEM((NC, 128, WIDTH), BF16),
        ]
        + [
            pltpu.VMEM((lead, ROWS3, 128), F32)
            for lead in (NXY, NXY, NXY, NXY, NZ, NXY)
        ]
        + [pltpu.SemaphoreType.DMA((21,)), pltpu.SemaphoreType.DMA((21,))],
        compiler_params=pltpu.CompilerParams(
            collective_id=0, has_side_effects=True, vmem_limit_bytes=VMEM_BYTES
        ),
        name="backward",
    )(*[pltpu.with_memory_space_constraint(a, pltpu.HBM) for a in args])
    outs = pl.pallas_call(
        functools.partial(hand_on, len(outs)),
        out_shape=out_shape,
        in_specs=[vmem] * 11,
        out_specs=(hbm,) * 11,
        scratch_shapes=[pltpu.SemaphoreType.DMA((11,))],
        name="hand_on",
    )(*[pltpu.with_memory_space_constraint(o, pltpu.VMEM) for o in outs])
    outs = list(outs)
    for n in (1, 2, 6):
        outs[n] = outs[n].reshape(-1)
    return tuple(outs)


def solution(mesh):
    by_point, by_rep = P(("pts", "rep"), None), P("rep", None)
    in_specs = (by_point, by_point) + (P(),) * 10
    out_specs = (by_point, P(), P(), by_rep, by_rep, P(), P(), P(), P(), P(), by_rep)
    return jax.shard_map(shards, mesh=mesh, in_specs=in_specs, out_specs=out_specs, check_vma=False)
```

```python
import functools

import jax
import jax.numpy as jnp
from jax import lax
from jax.experimental import pallas as pl
from jax.experimental.pallas import tpu as pltpu
from jax.sharding import PartitionSpec as P

MESH = pl.DeviceIdType.MESH
F32, BF16 = jnp.float32, jnp.bfloat16
HI = lax.Precision.HIGHEST

HEADS, SLICES, DIM = 8, 64, 32
WIDTH = HEADS * DIM
COLS = HEADS * SLICES
NX, NY, NZ, NC = 4, 4, 16, 2
NXY = NX * NY
ROWS1, ROWS2, ROWS3 = 9, 16, 3
SMALL = 40
VMEM_BYTES = 48 * 1024 * 1024
BF_MAX = 3.3895314e38


def dot(a, b, ca=1, cb=0, precision=None):
    return lax.dot_general(
        a, b, (((ca,), (cb,)), ((), ())), preferred_element_type=F32, precision=precision
    )


def iota(shape, dim):
    return lax.broadcasted_iota(jnp.int32, shape, dim)


def split(values):
    high = values.astype(BF16)
    return high, (values - high.astype(F32)).astype(BF16)


def group_sum(high, low, ones):
    parts = []
    for g in range(0, COLS, 256):
        parts.append(dot(high[:, g : g + 256], ones) + dot(low[:, g : g + 256], ones))
    return jnp.concatenate(parts, axis=1)


def block_diagonal(tile_t):
    whole = jnp.concatenate([tile_t] * HEADS, axis=0)
    own = iota((WIDTH, COLS), 0) // DIM == iota((WIDTH, COLS), 1) // SLICES
    return jnp.where(own, whole, 0.0)


def diagonal_rows(full):
    left = iota((DIM, 128), 1) < SLICES
    parts = []
    for g in range(HEADS // 2):
        cols = slice(128 * g, 128 * g + 128)
        parts.append(
            jnp.where(
                left,
                full[2 * DIM * g : 2 * DIM * g + DIM, cols],
                full[2 * DIM * g + DIM : 2 * DIM * g + 2 * DIM, cols],
            )
        )
    return parts


def thirds(values):
    first = values.astype(BF16)
    rest = values - first.astype(F32)
    second = rest.astype(BF16)
    return first, second, (rest - second.astype(F32)).astype(BF16)


def left_terms(parts, axis=0):
    a, b, c = parts
    return jnp.concatenate([a, a, b, a, b, c], axis=axis)


def right_terms(parts, axis=0):
    a, b, c = parts
    return jnp.concatenate([a, b, a, c, b, a], axis=axis)


def weight_terms(weights):
    terms = [part.astype(F32) for part in thirds(weights)]
    return left_terms(terms, 1).astype(BF16)


def pair_dot(left, right, cb):
    a, b = split(left)
    c, d = split(right)
    return dot(jnp.concatenate([a, a, b], axis=1), jnp.concatenate([c, d, c], axis=cb), 1, cb)


def token_step(totals, masses, d_mixed, forward_terms, backward_terms):
    scale = DIM ** (-0.5)
    inv = 1.0 / (masses + 1e-05)
    tokens = totals * inv
    qkv = dot(forward_terms, right_terms(thirds(tokens)))
    q, k, v = qkv[:DIM], qkv[DIM : 2 * DIM], qkv[2 * DIM :]
    q_terms, k_terms = left_terms(thirds(q)), right_terms(thirds(k))
    m_terms, v_terms = left_terms(thirds(d_mixed)), right_terms(thirds(v))
    same = iota((128, 128), 0) // SLICES == iota((128, 128), 1) // SLICES
    mixed, dq, dk, dv = [], [], [], []
    for g in range(HEADS // 2):
        cols = slice(128 * g, 128 * g + 128)
        scores = dot(q_terms[:, cols], k_terms[:, cols], 0, 0) * scale
        d_att = dot(m_terms[:, cols], v_terms[:, cols], 0, 0)
        powers = jnp.where(same, jnp.exp(scores), 0.0)
        att = powers / jnp.sum(powers, axis=1, keepdims=True)
        d_scores = att * (d_att - jnp.sum(d_att * att, axis=1, keepdims=True)) * scale
        mixed.append(pair_dot(v[:, cols], att, 1))
        dq.append(pair_dot(k[:, cols], d_scores, 1))
        dk.append(pair_dot(q[:, cols], d_scores, 0))
        dv.append(pair_dot(d_mixed[:, cols], att, 0))
    mixed = jnp.concatenate(mixed, axis=1)
    backs = [jnp.concatenate(d, axis=1) for d in (dq, dk, dv)]
    d_tokens = dot(
        backward_terms, jnp.concatenate([right_terms(thirds(d)) for d in backs], axis=0)
    )
    d_masses = -jnp.sum(d_tokens * tokens, axis=0, keepdims=True) * inv
    return mixed, d_tokens * inv, d_masses, tokens, backs


def far_first(a):
    return (2 - a + 3 * (a // 2) - 2 * (a // 3)) % 4


def kernel(
    everyone,
    chunk,
    points_h,
    out_grad_h,
    gain_h,
    bias_h,
    w_mid_h,
    w_feat_h,
    w_slice_h,
    temper_h,
    wq_h,
    wk_h,
    wv_h,
    w_out_h,
    o_points,
    o_gain,
    o_bias,
    o_mid,
    o_feat,
    o_slice,
    o_temper,
    o_q,
    o_k,
    o_v,
    o_out,
    points,
    out_grad,
    gain_ref,
    bias_ref,
    w_mid,
    w_feat,
    w_slice,
    temper,
    wq,
    wk,
    wv,
    w_out,
    loads,
    xhat_s,
    rstd_s,
    normed_s,
    mid_s,
    fd_s,
    low_s,
    logits_s,
    w_s,
    sw_s,
    sc_s,
    dmf_s,
    dn_s,
    p1,
    r11,
    r12,
    r13,
    pb,
    rb0,
    ab,
    rb1,
    rb2,
    rb3,
    pp,
    rp0,
    ap,
    rp1,
    sp,
    rp2,
    rp3,
    rp4,
    mb_s,
    tb_s,
    ps,
    rs0,
    as_,
    rs1,
    rs2,
    rs3,
    sends,
    recvs,
):
    held = (
        (points_h, points),
        (w_mid_h, w_mid),
        (w_feat_h, w_feat),
        (gain_h, gain_ref),
        (bias_h, bias_ref),
        (w_slice_h, w_slice),
        (temper_h, temper),
        (out_grad_h, out_grad),
        (w_out_h, w_out),
        (wq_h, wq),
        (wk_h, wk),
        (wv_h, wv),
    )
    copies = [pltpu.make_async_copy(a, b, loads.at[n]) for n, (a, b) in enumerate(held)]
    for copy in copies:
        copy.start()

    p, c = lax.axis_index("pts"), lax.axis_index("rep")
    x, y, z = p // (NY * NZ), p // NZ % NY, p % NZ
    xy = x * NY + y
    rows = points.shape[0]

    def plane_index(i):
        return (x + far_first(i // 4)) % NX * NY + (y + far_first(i % 4)) % NY

    def plane(i):
        return (plane_index(i) * NZ + z, c)

    def plane_cores(i):
        return (plane_index(i // 2) * NZ + z, (c + 1 + i % 2) % NC)

    def column_index(i):
        return (z + 8 + (i + 1) // 2 * (1 - 2 * (i % 2))) % NZ

    def column(i):
        return (xy * NZ + column_index(i), c)

    sibling = (p, 1 - c)
    barrier = pltpu.get_barrier_semaphore()

    greetings = [(plane_cores, i) for i in range(2 * NXY - 1)]
    greetings += [(column, i) for i in range(NZ - 1)]
    n_greetings = len(greetings)

    def greet(count):
        for who, i in greetings[:count]:
            pl.semaphore_signal(barrier, inc=1, device_id=who(i), device_id_type=MESH)
        del greetings[:count]

    with jax.named_scope("greet"):
        greet(n_greetings)

    unsent = []

    def pack(ref, grad):
        for h in range(NC):
            for l in range(2):
                ref[h, 8 * l : 8 * l + 8, 0:16, :] = grad[
                    128 * h : 128 * h + 128, 128 * l : 128 * l + 128
                ].reshape(8, 16, 128)

    def unpack(ref, out):
        for l in range(2):
            out[:, 128 * l : 128 * l + 128] = ref[8 * l : 8 * l + 8, 0:16, :].reshape(128, 128)

    def send_all(stage, who, count, src, dst):
        def body(i, _):
            pltpu.make_async_remote_copy(
                src(i), dst, sends.at[stage], recvs.at[stage], device_id=who(i), device_id_type=MESH
            ).start()
            return 0

        for i in range(count):
            body(i, 0)

    def swap(stage, src, dst):
        send_all(stage, lambda i: sibling, 1, lambda i: src, dst)

    def wait(stage, ref):
        copy = pltpu.make_async_remote_copy(
            ref, ref, sends.at[stage], recvs.at[stage], device_id=sibling, device_id_type=MESH
        )
        copy.wait_recv()
        unsent.append(copy)

    ones = (iota((256, 256), 0) // SLICES == iota((256, 256), 1) // SLICES).astype(F32).astype(BF16)

    with jax.named_scope("load"):
        for copy in copies[:7]:
            copy.wait()
    gain, bias = gain_ref[...], bias_ref[...]
    head_of = iota((1, COLS), 1) // SLICES
    temper_row = jnp.zeros((1, COLS), F32)
    for h in range(HEADS):
        temper_row = jnp.where(head_of == h, temper[:, h : h + 1], temper_row)
    inv_t = 1.0 / temper_row
    ws = w_slice[...].astype(F32)
    slice_blocks = block_diagonal(jnp.concatenate([ws] * HEADS, axis=1)).astype(BF16)

    with jax.named_scope("front"):
        for r in range(0, rows, chunk):
            here = pl.ds(r, chunk)
            xs = points[here, :].astype(F32)
            center = xs - jnp.mean(xs, axis=1, keepdims=True)
            rstd = lax.rsqrt(jnp.mean(center * center, axis=1, keepdims=True) + 1e-05)
            xhat = center * rstd
            xhat_s[here, :] = xhat
            rstd_s[here, :] = jnp.broadcast_to(rstd, (chunk, 128))
            normed = (xhat * gain + bias).astype(BF16)
            normed_s[here, :] = normed
            mid = dot(normed, w_mid[...]).astype(BF16)
            mid_s[here, :] = mid
            fd_s[here, WIDTH:] = dot(normed, w_feat[...]).astype(BF16)
            logits = dot(mid, slice_blocks) * inv_t
            logits_s[here, :] = logits
            powers = jnp.exp(logits)
            high = jnp.minimum(powers, BF_MAX).astype(BF16)
            low = (powers - high.astype(F32)).astype(BF16)
            weights = powers / group_sum(high, low, ones)
            w_s[here, :] = weights
            sw_s[here, :] = weights.astype(BF16)
        for copy in copies[7:]:
            copy.wait()
        for r in range(0, rows, chunk):
            here = pl.ds(r, chunk)
            d_high, d_low = split(dot(out_grad[here, :], w_out[...], 1, 1))
            fd_s[here, :WIDTH] = d_high
            low_s[here, :] = d_low

    with jax.named_scope("shares1"):
        sw = sw_s[...]
        by_fd = dot(fd_s[...], sw, 0, 0)
        by_low = dot(low_s[...], sw, 0, 0)
        tot = diagonal_rows(by_fd[WIDTH:])
        dmx = diagonal_rows(by_fd[:WIDTH] + by_low)
        mass = dot(jnp.ones((8, rows), BF16), sw)[:1]
        quarter = iota((1, 128), 1) // DIM
        for i in range(4):
            for j in range(4):
                k = 4 * i + j
                p1[0, k, 0:8, :] = tot[j][8 * i : 8 * i + 8]
                p1[1, k, 0:8, :] = dmx[j][8 * i : 8 * i + 8]
                p1[0, k, 8:9, :] = jnp.where(quarter == i, mass[:, 128 * j : 128 * j + 128], 0.0)
                p1[1, k, 8:9, :] = jnp.zeros((1, 128), F32)

    with jax.named_scope("barrier"):
        pl.semaphore_wait(barrier, n_greetings)

    me1 = c * NXY + xy
    with jax.named_scope("sum1_plane"):
        send_all(
            1,
            plane_cores,
            2 * NXY - 1,
            lambda i: p1.at[(c + 1 + i % 2) % NC, plane_index(i // 2)],
            r11.at[me1],
        )
        r11[me1] = p1[c, xy]
        projected = dot(out_grad[...], sw, 0, 0)
        by_normed = dot(normed_s[...], sw, 0, 0)
        for h in range(NC):
            half = projected[:, WIDTH * h : WIDTH * h + WIDTH]
            pp[h, :, 0:16, :] = half.reshape(NXY, 16, WIDTH)
            for l in range(2):
                half = by_normed[128 * h : 128 * h + 128, WIDTH * l : WIDTH * l + WIDTH]
                pp[h, :, 16 + 8 * l : 24 + 8 * l, :] = half.reshape(NXY, 8, WIDTH)
        swap(13, pp.at[1 - c], rp0)
        token_weights = (wq[...], wk[...], wv[...])
        forward_terms = jnp.concatenate([weight_terms(w.T) for w in token_weights], axis=0)
        backward_terms = jnp.concatenate([weight_terms(w) for w in token_weights], axis=1)
        wait(1, r11.at[pl.ds(0, 2 * NXY - 1)])
        r12[z] = jnp.sum(r11[...], axis=0)
    with jax.named_scope("sum1_column"):
        send_all(2, column, NZ - 1, lambda i: r12.at[z], r12.at[z])
        wait(13, rp0)
        ap[...] = pp[c] + rp0[...]
        send_all(14, plane, NXY - 1, lambda i: ap.at[plane_index(i)], rp1.at[xy])
        rp1[xy] = ap[xy]
        wait(2, r12.at[pl.ds(0, NZ - 1)])
        r13[me1] = jnp.sum(r12[...], axis=0)
    with jax.named_scope("sum1_back"):
        send_all(3, plane_cores, 2 * NXY - 1, lambda i: r13.at[me1], r13.at[me1])
        wait(14, rp1.at[pl.ds(0, NXY - 1)])
        piece = jnp.sum(rp1[...], axis=0)
        for k in range(NZ):
            sp[k, 0:1] = piece[k : k + 1]
            sp[k, 1:2] = piece[16 + k : 17 + k]
        send_all(15, column, NZ - 1, lambda i: sp.at[column_index(i)], rp2.at[z])
        rp2[z] = sp[z]
        wait(3, r13.at[pl.ds(0, 2 * NXY - 1)])

    def whole(half):
        return jnp.concatenate(
            [
                jnp.concatenate([r13[NXY * half + 4 * i + j, 0:8, :] for i in range(4)], axis=0)
                for j in range(4)
            ],
            axis=1,
        )

    with jax.named_scope("tokens"):
        masses = jnp.concatenate(
            [sum(r13[4 * i + j, 8:9, :] for i in range(4)) for j in range(4)], axis=1
        )
        mixed, d_totals, d_masses, tokens, backs = token_step(
            whole(0), masses, whole(1), forward_terms, backward_terms
        )
        mixed_blocks = block_diagonal(mixed.astype(BF16).astype(F32)).astype(BF16)
        totals_blocks = block_diagonal(d_totals.astype(BF16).astype(F32)).astype(BF16)
        both = jnp.concatenate([mixed_blocks, totals_blocks], axis=0)
        for h in range(NC):
            part = (slice(128 * h, 128 * h + 128), slice(WIDTH * h, WIDTH * h + WIDTH))
            mb_s[h] = mixed_blocks[part]
            tb_s[h] = totals_blocks[part]

    w_both = jnp.concatenate([w_mid[...], w_feat[...]], axis=1)

    def fold(values):
        return jnp.sum(values.reshape(values.shape[0] // 8, 8, values.shape[1]), axis=0)

    sums = [jnp.zeros((8, COLS), F32), jnp.zeros((8, WIDTH), F32), jnp.zeros((8, WIDTH), F32)]

    def back(r):
        here = pl.ds(r, chunk)
        weights = w_s[here, :]
        d_weights = dot(fd_s[here, :], both) + d_masses
        high, low = split(d_weights * weights)
        d_logits = weights * (d_weights - group_sum(high, low, ones))
        scaled = (d_logits * inv_t).astype(BF16)
        sc_s[here, :] = scaled
        sums[0] += fold(d_logits * logits_s[here, :])
        dmf_s[here, :WIDTH] = dot(scaled, slice_blocks, 1, 1).astype(BF16)

    def norm(r):
        here = pl.ds(r, chunk)
        dmf_s[here, WIDTH:] = dot(sw_s[here, :], totals_blocks, 1, 1).astype(BF16)
        d_normed = dot(dmf_s[here, :], w_both, 1, 1)
        dn_s[here, :] = d_normed
        sums[1] += fold(d_normed * xhat_s[here, :])
        sums[2] += fold(d_normed)

    with jax.named_scope("back"):
        for r in range(0, rows, chunk):
            back(r)
    with jax.named_scope("sumb_core"):
        pack(pb, dot(normed_s[...], dmf_s[:, :WIDTH], 0, 0))
        swap(9, pb.at[1 - c], rb0)
        for r in range(0, rows // 2, chunk):
            norm(r)
    with jax.named_scope("shares_small"):
        for r in range(rows // 2, rows, chunk):
            norm(r)
        slice_sum = sum(diagonal_rows(dot(mid_s[...], sc_s[...], 0, 0)))
        temper_sum, gain_sum, bias_sum = (jnp.sum(v, axis=0, keepdims=True) for v in sums)
        small = [gain_sum[:, 128 * l : 128 * l + 128] for l in range(2)]
        small += [bias_sum[:, 128 * l : 128 * l + 128] for l in range(2)]
        small += [temper_sum[:, 128 * l : 128 * l + 128] for l in range(4)]
        small += [slice_sum, jnp.zeros((ROWS3 * NXY - SMALL, 128), F32)]
        small = jnp.concatenate(small, axis=0)
        for k in range(NXY):
            ps[k] = small[ROWS3 * k : ROWS3 * k + ROWS3]
        swap(0, ps, rs0)

    with jax.named_scope("sumb_plane"):
        wait(9, rb0)
        ab[...] = pb[c] + rb0[...]
        send_all(10, plane, NXY - 1, lambda i: ab.at[plane_index(i)], rb1.at[xy])
        rb1[xy] = ab[xy]

    with jax.named_scope("out_feat"):
        wait(15, rp2.at[pl.ds(0, NZ - 1)])
        summed = jnp.sum(rp2[...], axis=0)
        for n, blocks in enumerate((mb_s[c], tb_s[z // 8])):
            row_high, row_low = split(jnp.broadcast_to(summed[n : n + 1], (16, WIDTH)))
            own = dot(row_high, blocks, 1, 1) + dot(row_low, blocks, 1, 1)
            rp3[z, n : n + 1] = own[:1] / everyone
        send_all(16, column, NZ - 1, lambda i: rp3.at[z], rp3.at[z])

    with jax.named_scope("small_plane"):
        wait(0, rs0)
        as_[...] = ps[...] + rs0[...]
        send_all(18, plane, NXY - 1, lambda i: as_.at[plane_index(i)], rs1.at[xy])
        rs1[xy] = as_[xy]
    with jax.named_scope("sumb_column"):
        wait(10, rb1.at[pl.ds(0, NXY - 1)])
        rb2[z] = jnp.sum(rb1[...], axis=0)
        send_all(11, column, NZ - 1, lambda i: rb2.at[z], rb2.at[z])
    with jax.named_scope("points"):
        for r in range(0, rows, chunk):
            here = pl.ds(r, chunk)
            xhat = xhat_s[here, :]
            d_xhat = dn_s[here, :] * gain
            inner = d_xhat - jnp.mean(d_xhat, axis=1, keepdims=True)
            inner = inner - xhat * jnp.mean(d_xhat * xhat, axis=1, keepdims=True)
            o_points[here, :] = (inner * rstd_s[here, 0:1]).astype(BF16)

    with jax.named_scope("small_column"):
        wait(18, rs1.at[pl.ds(0, NXY - 1)])
        rs2[z] = jnp.sum(rs1[...], axis=0)
        send_all(19, column, NZ - 1, lambda i: rs2.at[z], rs2.at[z])
    with jax.named_scope("out_column"):
        wait(16, rp3.at[pl.ds(0, NZ - 1)])
        for n in range(2):
            rp4[xy, n] = jnp.concatenate([rp3[k, n : n + 1] for k in range(NZ)], axis=0)
        send_all(17, plane, NXY - 1, lambda i: rp4.at[xy], rp4.at[xy])
    with jax.named_scope("token_grads"):
        for out, grad in zip((o_q, o_k, o_v), backs):
            out[...] = dot(tokens, grad, 1, 1, HI) / everyone
    with jax.named_scope("sumb_back"):
        wait(11, rb2.at[pl.ds(0, NZ - 1)])
        rb3[xy] = jnp.sum(rb2[...], axis=0) / everyone
        send_all(12, plane, NXY - 1, lambda i: rb3.at[xy], rb3.at[xy])
    with jax.named_scope("small_back"):
        wait(19, rs2.at[pl.ds(0, NZ - 1)])
        rs3[xy] = jnp.sum(rs2[...], axis=0) / everyone
        send_all(20, plane, NXY - 1, lambda i: rs3.at[xy], rs3.at[xy])
    with jax.named_scope("out_last"):
        wait(17, rp4.at[pl.ds(0, NXY - 1)])
        o_out[...] = rp4[:, 0].reshape(WIDTH, 128).T
        for l in range(2):
            o_feat[:, 128 * l : 128 * l + 128] = rp4[:, 1, 8 * l : 8 * l + 8, :].reshape(128, 128)
    with jax.named_scope("small_last"):
        wait(20, rs3.at[pl.ds(0, NXY - 1)])
        small = [rs3[k // ROWS3, k % ROWS3 : k % ROWS3 + 1, :] for k in range(SMALL)]
        for l in range(2):
            o_gain[:, 128 * l : 128 * l + 128] = small[l]
            o_bias[:, 128 * l : 128 * l + 128] = small[2 + l]
        folded = jnp.concatenate(small[8:], axis=0)
        o_slice[...] = (folded + pltpu.roll(folded, SLICES, 1))[:, :SLICES]
        lane, place = iota((1, 128), 1), iota((1, HEADS), 1)
        d_temper = jnp.zeros((1, HEADS), F32)
        for g in range(4):
            for s in range(2):
                part = jnp.where(lane // SLICES == s, small[4 + g], 0.0)
                part = jnp.sum(part, axis=1, keepdims=True)
                d_temper = jnp.where(place == 2 * g + s, part, d_temper)
        o_temper[...] = -d_temper / temper[...]
    with jax.named_scope("sumb_last"):
        wait(12, rb3.at[pl.ds(0, NXY - 1)])
        unpack(rb3, o_mid)

    with jax.named_scope("done"):
        for copy in unsent:
            copy.wait_send()


def hand_on(count, *refs):
    sems = refs[2 * count]
    copies = [pltpu.make_async_copy(refs[n], refs[count + n], sems.at[n]) for n in range(count)]
    for copy in copies:
        copy.start()
    for copy in copies:
        copy.wait()


def shards(
    points, out_grad, ln_gain, ln_bias, w_mid, w_feat, w_slice, temper, wq, wk, wv, w_out
):
    rows = points.shape[0]
    everyone = rows * NXY * NZ * NC
    hbm = pl.BlockSpec(memory_space=pltpu.HBM)
    vmem = pl.BlockSpec(memory_space=pltpu.VMEM)
    f = lambda *s: jax.ShapeDtypeStruct(s, F32)
    args = (
        points,
        out_grad,
        ln_gain.reshape(1, -1),
        ln_bias.reshape(1, -1),
        w_mid,
        w_feat,
        w_slice,
        temper.reshape(1, -1),
        wq,
        wk,
        wv,
        w_out,
    )
    out_shape = (
        jax.ShapeDtypeStruct((rows, WIDTH), BF16),
        f(1, WIDTH),
        f(1, WIDTH),
        f(128, WIDTH),
        f(128, WIDTH),
        f(DIM, SLICES),
        f(1, HEADS),
        f(DIM, DIM),
        f(DIM, DIM),
        f(DIM, DIM),
        f(128, WIDTH),
    )
    outs = pl.pallas_call(
        functools.partial(kernel, float(everyone), 256),
        out_shape=out_shape,
        in_specs=[hbm] * 12,
        out_specs=(vmem,) * 11,
        scratch_shapes=[pltpu.VMEM(a.shape, a.dtype) for a in args]
        + [pltpu.SemaphoreType.DMA((12,))]
        + [
            pltpu.VMEM((rows, WIDTH), F32),
            pltpu.VMEM((rows, 128), F32),
            pltpu.VMEM((rows, WIDTH), BF16),
            pltpu.VMEM((rows, WIDTH), BF16),
            pltpu.VMEM((rows, 2 * WIDTH), BF16),
            pltpu.VMEM((rows, WIDTH), BF16),
            pltpu.VMEM((rows, COLS), F32),
            pltpu.VMEM((rows, COLS), F32),
            pltpu.VMEM((rows, COLS), BF16),
            pltpu.VMEM((rows, COLS), BF16),
            pltpu.VMEM((rows, 2 * WIDTH), BF16),
            pltpu.VMEM((rows, WIDTH), F32),
        ]
        + [
            pltpu.VMEM(lead + (ROWS1, 128), F32)
            for lead in ((NC, NXY), (NC * NXY,), (NZ,), (NC * NXY,))
        ]
        + [
            pltpu.VMEM(lead + (ROWS2, 128), F32)
            for lead in ((NC, NXY), (NXY,), (NXY,), (NXY,), (NZ,), (NXY,))
        ]
        + [
            pltpu.VMEM((NC, NXY, 32, WIDTH), F32),
            pltpu.VMEM((NXY, 32, WIDTH), F32),
            pltpu.VMEM((NXY, 32, WIDTH), F32),
            pltpu.VMEM((NXY, 32, WIDTH), F32),
            pltpu.VMEM((NZ, 2, WIDTH), F32),
            pltpu.VMEM((NZ, 2, WIDTH), F32),
            pltpu.VMEM((NZ, 2, 128), F32),
            pltpu.VMEM((NXY, 2, 16, 128), F32),
            pltpu.VMEM((NC, 128, WIDTH), BF16),
            pltpu.VMEM((NC, 128, WIDTH), BF16),
        ]
        + [
            pltpu.VMEM((lead, ROWS3, 128), F32)
            for lead in (NXY, NXY, NXY, NXY, NZ, NXY)
        ]
        + [pltpu.SemaphoreType.DMA((21,)), pltpu.SemaphoreType.DMA((21,))],
        compiler_params=pltpu.CompilerParams(
            collective_id=0, has_side_effects=True, vmem_limit_bytes=VMEM_BYTES
        ),
        name="backward",
    )(*[pltpu.with_memory_space_constraint(a, pltpu.HBM) for a in args])
    outs = pl.pallas_call(
        functools.partial(hand_on, len(outs)),
        out_shape=out_shape,
        in_specs=[vmem] * 11,
        out_specs=(hbm,) * 11,
        scratch_shapes=[pltpu.SemaphoreType.DMA((11,))],
        name="hand_on",
    )(*[pltpu.with_memory_space_constraint(o, pltpu.VMEM) for o in outs])
    outs = list(outs)
    for n in (1, 2, 6):
        outs[n] = outs[n].reshape(-1)
    return tuple(outs)


def solution(mesh):
    by_point, by_rep = P(("pts", "rep"), None), P("rep", None)
    in_specs = (by_point, by_point) + (P(),) * 10
    out_specs = (by_point, P(), P(), by_rep, by_rep, P(), P(), P(), P(), P(), by_rep)
    return jax.shard_map(shards, mesh=mesh, in_specs=in_specs, out_specs=out_specs, check_vma=False)
```
